32 devices in a mesh: blk: 4 (over y, x), uly: 8 (over z, core).
Axes of the slice: x: 2, y: 2, z: 4, core: 2. Of those that a mesh axis runs over, the one named last changes fastest.
Arguments:
- queries: bfloat16 [4096, 4096], P(('blk', 'uly')), may hold values from -1.5 to 1.5
- keys: bfloat16 [4096, 1024], P(('blk', 'uly')), may hold values from -1.5 to 1.5
- values: bfloat16 [4096, 1024], P(('blk', 'uly')), may hold values from -6 to 6
- grad_out: bfloat16 [4096, 4096], P(('blk', 'uly')), may hold values from -96 to 96
- row_lse: float32 [4096, 32], P('blk', 'uly'), may hold values from 6 to 7.5
- row_delta: float32 [4096, 32], P('blk', 'uly'), may hold values from -960 to 960
- pattern: int32 [32, 2], replicated, may hold values from 0 to 31, as said below
- memory_keys: bfloat16 [128, 4096], P(None, 'uly'), may hold values from -1.5 to 1.5
- memory_values: bfloat16 [128, 4096], P(None, 'uly'), may hold values from -6 to 6
Outputs:
- grad_queries: bfloat16 [4096, 4096], P(('blk', 'uly'))
- grad_keys: float32 [4096, 1024], P(('blk', 'uly'))
- grad_values: float32 [4096, 1024], P(('blk', 'uly'))
- grad_memory_keys: float32 [128, 4096], P(None, 'uly')
- grad_memory_values: float32 [128, 4096], P(None, 'uly')
The draws below stay inside these ranges and needn't reach their ends.
Inputs may be any that keep to these rules, and one draw needn't show every extreme that they name: `pattern`: query block b lies in span b // 8. The rows of one span name exactly one block of every span that is neither that span nor beside it; all their other named blocks lie in the span itself.
All inputs are finite; a program needn't handle non-finite values.
Results may differ from the reference program's by a relative error of at most 0.0085.
Values may be sent and summed in bfloat16 or wider, within the bound.
No kernel may reach another device: no remote copies, remote signals or barrier semaphores. Data moves between devices by JAX's collectives and lax.ppermute only.
A program may use at most 64 MiB of HBM per device.

```python
import jax
import jax.numpy as jnp
from jax import lax

QUERY_HEADS = 32
KEY_HEADS = 8
HEAD_FEATURES = 128
BLOCK = 128
RANDOM = 2
QUERY_PER_KEY = 4
QB_DEV = 8
SPANS = 4
SEQUENCE_TOKENS = 4096
NBLOCKS = 32


def draw_pattern(key, part):
    entries = QB_DEV * RANDOM

    def for_span(span_id, span_key):
        key_a, key_b = jax.random.split(span_key, 2)
        entry_ids = jnp.arange(entries, dtype=jnp.int32)
        left_count = jnp.maximum(span_id - 1, 0)
        far_count = SPANS - 1 - (span_id > 0).astype(jnp.int32) - (span_id < SPANS - 1).astype(jnp.int32)
        far_owner = jnp.where(entry_ids < left_count, entry_ids, entry_ids - left_count + span_id + 2)
        owners = jnp.where(entry_ids < far_count, far_owner, span_id)
        blocks = jax.random.randint(key_a, (entries,), 0, QB_DEV)
        picked = owners * QB_DEV + blocks
        shuffled = jax.random.permutation(key_b, entries)
        return picked[shuffled].reshape(QB_DEV, RANDOM)
    span_ids = jnp.arange(SPANS, dtype=jnp.int32)
    span_keys = jax.random.split(key, SPANS)
    all_rows = jax.vmap(for_span)(span_ids, span_keys)
    return all_rows.reshape(NBLOCKS, RANDOM).astype(jnp.int32)


def block_scale(stream_key, extent, cuts, least, high):
    level = 1.0
    for axis_at, shards_of in cuts:
        draws = jax.random.uniform(jax.random.fold_in(jax.random.fold_in(stream_key, 6), axis_at), (shards_of,), jnp.float32, least / len(cuts), high / len(cuts))
        level = level * jnp.repeat(jnp.exp(draws), extent[axis_at] // shards_of).reshape((-1,) + (1,) * (len(extent) - 1 - axis_at))
    return level


def gaussian(stream_key, dims, deviation, limit, pieces=(), kind=jnp.bfloat16):
    drawn = deviation * jax.random.normal(stream_key, dims, jnp.float32)
    if pieces:
        drawn = drawn * block_scale(stream_key, dims, pieces, -0.22, 0.18)
    return jnp.clip(drawn, -limit, limit).astype(kind)


def setup_inputs(seed: int = 0) -> dict:
    key_of = jax.random.split(jax.random.key(seed), 10)
    queries = jnp.clip(jax.random.uniform(key_of[0], (SEQUENCE_TOKENS, QUERY_HEADS * HEAD_FEATURES), jnp.float32, -1.5, 1.5) * block_scale(key_of[0], (SEQUENCE_TOKENS, QUERY_HEADS * HEAD_FEATURES), ((0, 32),), -0.4, 0.0), -1.5, 1.5).astype(jnp.bfloat16)
    keys = jnp.clip(jax.random.uniform(key_of[1], (SEQUENCE_TOKENS, KEY_HEADS * HEAD_FEATURES), jnp.float32, -1.5, 1.5) * block_scale(key_of[1], (SEQUENCE_TOKENS, KEY_HEADS * HEAD_FEATURES), ((0, 32),), -0.4, 0.0), -1.5, 1.5).astype(jnp.bfloat16)
    values = gaussian(key_of[2], (SEQUENCE_TOKENS, KEY_HEADS * HEAD_FEATURES), 1.0, 6.0, ((0, 32),))
    grad_out = gaussian(key_of[3], (SEQUENCE_TOKENS, QUERY_HEADS * HEAD_FEATURES), 16.0, 96.0, ((0, 32),))
    row_lse = jnp.clip(6.0 + 1.5 * jax.random.uniform(key_of[4], (SEQUENCE_TOKENS, QUERY_HEADS), jnp.float32) ** block_scale(key_of[4], (SEQUENCE_TOKENS, QUERY_HEADS), ((0, 4), (1, 8)), -0.2, 0.2), 6.0, 7.5)
    row_delta = gaussian(key_of[5], (SEQUENCE_TOKENS, QUERY_HEADS), 160.0, 960.0, ((0, 4), (1, 8)), jnp.float32)
    pattern = draw_pattern(jax.random.fold_in(key_of[9], 71), 0)
    memory_keys = jnp.clip(jax.random.uniform(key_of[7], (BLOCK, QUERY_HEADS * HEAD_FEATURES), jnp.float32, -1.5, 1.5) * block_scale(key_of[7], (BLOCK, QUERY_HEADS * HEAD_FEATURES), ((1, 8),), -0.4, 0.0), -1.5, 1.5).astype(jnp.bfloat16)
    memory_values = gaussian(key_of[8], (BLOCK, QUERY_HEADS * HEAD_FEATURES), 1.0, 6.0, ((1, 8),))
    return dict(queries=queries, keys=keys, values=values, grad_out=grad_out, row_lse=row_lse, row_delta=row_delta, pattern=pattern, memory_keys=memory_keys, memory_values=memory_values)


def reference(queries, keys, values, grad_out, row_lse, row_delta, pattern, memory_keys, memory_values):
    score_scale = HEAD_FEATURES ** -0.5
    block_count = SEQUENCE_TOKENS // BLOCK
    block_ids = jnp.arange(block_count, dtype=jnp.int32)
    window = jnp.stack([block_ids - 1, block_ids, block_ids + 1], axis=1)
    window_ok = (window >= 0) & (window < block_count)
    key_index = jnp.concatenate([jnp.clip(window, 0, block_count - 1), pattern.astype(jnp.int32)], axis=1)
    pair_ok = jnp.concatenate([window_ok, jnp.ones((block_count, RANDOM + 1), dtype=bool)], axis=1).astype(jnp.float32)
    seq_terms = RANDOM + 3

    def columns(matrix, column_id):
        return lax.dynamic_slice_in_dim(matrix, column_id * HEAD_FEATURES, HEAD_FEATURES, 1).astype(jnp.float32)

    def per_head(head_id):
        group_id = head_id // QUERY_PER_KEY
        query_blk = columns(queries, head_id).reshape(block_count, BLOCK, HEAD_FEATURES)
        dout_blk = columns(grad_out, head_id).reshape(block_count, BLOCK, HEAD_FEATURES)
        key_rows = columns(keys, group_id).reshape(block_count, BLOCK, HEAD_FEATURES)
        value_rows = columns(values, group_id).reshape(block_count, BLOCK, HEAD_FEATURES)
        mem_key = columns(memory_keys, head_id)
        mem_value = columns(memory_values, head_id)
        key_sets = jnp.concatenate([key_rows[key_index], jnp.broadcast_to(mem_key, (block_count, 1, BLOCK, HEAD_FEATURES))], axis=1)
        value_sets = jnp.concatenate([value_rows[key_index], jnp.broadcast_to(mem_value, (block_count, 1, BLOCK, HEAD_FEATURES))], axis=1)
        lse_blk = lax.dynamic_slice_in_dim(row_lse, head_id, 1, 1).reshape(block_count, BLOCK)
        delta_blk = lax.dynamic_slice_in_dim(row_delta, head_id, 1, 1).reshape(block_count, BLOCK)
        scores = jnp.einsum('nad,nskd->nsak', query_blk, key_sets) * score_scale
        weights = jnp.exp(scores - lse_blk[:, None, :, None]) * pair_ok[:, :, None, None]
        dweights = jnp.einsum('nad,nskd->nsak', dout_blk, value_sets)
        dscores = weights * (dweights - delta_blk[:, None, :, None])
        weight_bf = lax.optimization_barrier(weights.astype(jnp.bfloat16)).astype(jnp.float32)
        dscore_bf = lax.optimization_barrier(dscores.astype(jnp.bfloat16)).astype(jnp.float32)
        grad_q = (jnp.einsum('nsak,nskd->nad', dscore_bf, key_sets) * score_scale).astype(jnp.bfloat16)
        key_term = jnp.einsum('nsak,nad->nskd', dscore_bf, query_blk) * score_scale
        key_term = lax.optimization_barrier(key_term.astype(jnp.bfloat16)).astype(jnp.float32)
        value_term = jnp.einsum('nsak,nad->nskd', weight_bf, dout_blk)
        value_term = lax.optimization_barrier(value_term.astype(jnp.bfloat16)).astype(jnp.float32)
        head_dk = jnp.zeros((block_count, BLOCK, HEAD_FEATURES), jnp.float32).at[key_index].add(key_term[:, :seq_terms])
        head_dv = jnp.zeros((block_count, BLOCK, HEAD_FEATURES), jnp.float32).at[key_index].add(value_term[:, :seq_terms])
        mem_dk = jnp.sum(key_term[:, seq_terms], axis=0)
        mem_dv = jnp.sum(value_term[:, seq_terms], axis=0)
        return (grad_q.reshape(SEQUENCE_TOKENS, HEAD_FEATURES), head_dk.astype(jnp.bfloat16).reshape(SEQUENCE_TOKENS, HEAD_FEATURES),
                head_dv.astype(jnp.bfloat16).reshape(SEQUENCE_TOKENS, HEAD_FEATURES), mem_dk, mem_dv)

    results = lax.map(per_head, jnp.arange(QUERY_HEADS, dtype=jnp.int32))
    grad_q_all, dk_heads, dv_heads, mk_heads, mv_heads = results
    grad_queries = grad_q_all.transpose(1, 0, 2).reshape(SEQUENCE_TOKENS, QUERY_HEADS * HEAD_FEATURES)

    def group_sum(stacked_parts, count_of_rows):
        summed_terms = jnp.sum(stacked_parts.astype(jnp.float32).reshape(KEY_HEADS, QUERY_PER_KEY, count_of_rows, HEAD_FEATURES), axis=1)
        return summed_terms.transpose(1, 0, 2).reshape(count_of_rows, KEY_HEADS * HEAD_FEATURES)

    def rows_by_head(stacked_parts):
        return stacked_parts.transpose(1, 0, 2).reshape(BLOCK, QUERY_HEADS * HEAD_FEATURES)

    return (grad_queries, group_sum(dk_heads, SEQUENCE_TOKENS), group_sum(dv_heads, SEQUENCE_TOKENS),
            rows_by_head(mk_heads), rows_by_head(mv_heads))
```

```python
import functools
import math

import jax
import jax.numpy as jnp
from jax import lax
from jax.experimental import pallas as pl
from jax.experimental.pallas import tpu as pltpu
from jax.sharding import PartitionSpec as P

QUERY_HEADS = 32
KEY_HEADS = 8
HEAD_FEATURES = 128
BLOCK = 128
RANDOM = 2
SEQ_PAIRS = RANDOM + 3
GROUP = QUERY_HEADS // KEY_HEADS
SCALE = HEAD_FEATURES ** (-0.5)
LOG2E = math.log2(math.e)
FAR = 1e30
NN = (((1,), (0,)), ((), ()))
NT = (((1,), (1,)), ((), ()))


def dot(left, right, dims=NN):
    return lax.dot_general(left, right, dims, preferred_element_type=jnp.float32)


def attention_kernel(
    index_ref,
    far_ref,
    qd_ref,
    kv_ref,
    slot_ref,
    stat_ref,
    mk_ref,
    mv_ref,
    dq_ref,
    acc_ref,
    dmk_ref,
    dmv_ref,
    kt_ref,
    mkt_ref,
):
    step = pl.program_id(0)
    block_count = kv_ref.shape[0]
    span_count = slot_ref.shape[0]
    heads = mk_ref.shape[1] // HEAD_FEATURES

    def col(head):
        return pl.ds(head * HEAD_FEATURES, HEAD_FEATURES)

    @pl.when(step == 0)
    def _():
        acc_ref[...] = jnp.zeros_like(acc_ref)
        dmk_ref[...] = jnp.zeros_like(dmk_ref)
        dmv_ref[...] = jnp.zeros_like(dmv_ref)
        for b in range(block_count):
            kt_ref[0, b] = kv_ref[b, 0]
            kt_ref[1, b] = kv_ref[b, 1]
            kt_ref[2, b] = kv_ref[b, 0].T
        for s in range(span_count):
            kt_ref[0, block_count + s] = slot_ref[s, 0]
            kt_ref[1, block_count + s] = slot_ref[s, 1]
            kt_ref[2, block_count + s] = slot_ref[s, 0].T
        for h in range(heads):
            mkt_ref[h] = mk_ref[:, col(h)].T

    index = [index_ref[step, j] for j in range(SEQ_PAIRS)]
    lse = stat_ref[0, 0:1, :] * LOG2E
    delta = stat_ref[0, 1:2, :]
    q_heads = [qd_ref[0, 0, :, col(h)] for h in range(heads)]
    do_heads = [qd_ref[0, 1, :, col(h)] for h in range(heads)]
    q_all = jnp.concatenate(q_heads, axis=0)
    do_all = jnp.concatenate(do_heads, axis=0)
    keys = jnp.concatenate([kt_ref[0, i] for i in index], axis=0)
    values = jnp.concatenate([kt_ref[1, i] for i in index], axis=0)
    keys_t = jnp.concatenate([kt_ref[2, i] for i in index], axis=1)

    def weigh(scores, dweights, lse_row):
        weights = jnp.exp2(scores * (SCALE * LOG2E) - lse_row)
        dscores = weights * (dweights - delta)
        return weights.astype(jnp.bfloat16), dscores.astype(jnp.bfloat16)

    scores = dot(keys, q_all, NT)
    dweights = dot(values, do_all, NT)
    parts = [
        weigh(
            scores[j * BLOCK : (j + 1) * BLOCK],
            dweights[j * BLOCK : (j + 1) * BLOCK],
            lse + far_ref[step, j],
        )
        for j in range(SEQ_PAIRS)
    ]
    weights = jnp.concatenate([w for w, _ in parts], axis=0)
    dscores = jnp.concatenate([d for _, d in parts], axis=0)
    dq_t = dot(keys_t, dscores)
    dk = dot(dscores, q_all)
    dv = dot(weights, do_all)
    for j, i in enumerate(index):
        rows = slice(j * BLOCK, (j + 1) * BLOCK)
        acc_ref[0, i] += dk[rows]
        acc_ref[1, i] += dv[rows]

    mem_scores = jnp.concatenate(
        [dot(mk_ref[:, col(h)], q_heads[h], NT) for h in range(heads)], axis=1
    )
    mem_dweights = jnp.concatenate(
        [dot(mv_ref[:, col(h)], do_heads[h], NT) for h in range(heads)], axis=1
    )
    mem_w, mem_d = weigh(mem_scores, mem_dweights, lse)
    for h in range(heads):
        lanes = slice(h * HEAD_FEATURES, (h + 1) * HEAD_FEATURES)
        dmk_ref[:, col(h)] += dot(mem_d[:, lanes], q_heads[h]) * SCALE
        dmv_ref[:, col(h)] += dot(mem_w[:, lanes], do_heads[h])
        head_dq = dq_t[:, lanes] + dot(mkt_ref[h], mem_d[:, lanes])
        dq_ref[0, :, col(h)] = (head_dq * SCALE).T.astype(jnp.bfloat16)


def attention(index, far, qd, kv, slots, stats, memory_keys, memory_values):
    block_count = qd.shape[0]
    width = qd.shape[3]
    pool = kv.shape[0] + slots.shape[0]
    whole = lambda shape: pl.BlockSpec(shape, lambda n, *_: (0,) * len(shape))
    pairs = block_count * (SEQ_PAIRS + 1) * width // HEAD_FEATURES
    return pl.pallas_call(
        attention_kernel,
        grid_spec=pltpu.PrefetchScalarGridSpec(
            num_scalar_prefetch=2,
            grid=(block_count,),
            in_specs=[
                pl.BlockSpec((1, 2, BLOCK, width), lambda n, *_: (n, 0, 0, 0)),
                whole(kv.shape),
                whole(slots.shape),
                pl.BlockSpec((1, 2, width), lambda n, *_: (n, 0, 0)),
                whole(memory_keys.shape),
                whole(memory_values.shape),
            ],
            out_specs=[
                pl.BlockSpec((1, BLOCK, width), lambda n, *_: (n, 0, 0)),
                whole((2, pool, BLOCK, HEAD_FEATURES)),
                whole((BLOCK, width)),
                whole((BLOCK, width)),
            ],
            scratch_shapes=[
                pltpu.VMEM((3, pool, BLOCK, HEAD_FEATURES), jnp.bfloat16),
                pltpu.VMEM((width // HEAD_FEATURES, BLOCK, HEAD_FEATURES), jnp.bfloat16),
            ],
        ),
        out_shape=[
            jax.ShapeDtypeStruct((block_count, BLOCK, width), jnp.bfloat16),
            jax.ShapeDtypeStruct((2, pool, BLOCK, HEAD_FEATURES), jnp.float32),
            jax.ShapeDtypeStruct((BLOCK, width), jnp.float32),
            jax.ShapeDtypeStruct((BLOCK, width), jnp.float32),
        ],
        compiler_params=pltpu.CompilerParams(vmem_limit_bytes=48 * 1024 * 1024),
        cost_estimate=pl.CostEstimate(
            flops=pairs * 10 * BLOCK * BLOCK * HEAD_FEATURES,
            bytes_accessed=8 * 1024 * 1024,
            transcendentals=pairs * BLOCK * BLOCK,
        ),
    )(index, far, qd, kv, slots, stats, memory_keys, memory_values)


def pair_tables(pattern, span_count, block_count, my_span):
    entries = block_count * RANDOM
    flat_pattern = pattern.reshape(span_count, entries)
    owner_all = flat_pattern // block_count
    local_all = flat_pattern % block_count
    span_ids = jnp.arange(span_count, dtype=jnp.int32)
    near_span = jnp.abs(span_ids - my_span) == 1
    from_me = (owner_all == my_span) & (span_ids != my_span)[:, None]
    named_block = jnp.sum(jnp.where(from_me, local_all, 0), axis=1)
    edge_block = jnp.where(span_ids > my_span, block_count - 1, 0)
    send_block = jnp.where(near_span, edge_block, named_block)
    my_pattern = lax.dynamic_slice_in_dim(flat_pattern, my_span, 1, 0)[0]
    my_owner = my_pattern // block_count
    random_index = jnp.where(my_owner == my_span, my_pattern % block_count, block_count + my_owner)
    random_index = random_index.reshape(block_count, RANDOM)
    block_ids = jnp.arange(block_count, dtype=jnp.int32)
    left_index = jnp.where(block_ids > 0, block_ids - 1, block_count + jnp.maximum(my_span - 1, 0))
    right_index = jnp.where(
        block_ids < block_count - 1,
        block_ids + 1,
        block_count + jnp.minimum(my_span + 1, span_count - 1),
    )
    pair_index = jnp.concatenate(
        [left_index[:, None], block_ids[:, None], right_index[:, None], random_index], axis=1
    )
    left_far = jnp.where((block_ids > 0) | (my_span > 0), 0.0, FAR)
    right_far = jnp.where((block_ids < block_count - 1) | (my_span < span_count - 1), 0.0, FAR)
    none = jnp.zeros((block_count,), jnp.float32)
    pair_far = jnp.stack([left_far, none, right_far, none, none], axis=1).astype(jnp.float32)
    return send_block, pair_index, pair_far


def shards(
    queries, keys, values, grad_out, row_lse, row_delta, pattern, memory_keys, memory_values
):
    span_count = lax.axis_size("blk")
    head_ways = lax.axis_size("uly")
    my_span = lax.axis_index("blk")
    present_rows = queries.shape[0]
    span_rows = present_rows * head_ways
    block_count = span_rows // BLOCK
    local_heads = QUERY_HEADS // head_ways
    width = local_heads * HEAD_FEATURES
    copies = GROUP // local_heads

    send_block, pair_index, pair_far = pair_tables(pattern, span_count, block_count, my_span)

    def pieces(rows, piece_width):
        return rows.reshape(present_rows, -1, piece_width).transpose(1, 0, 2)

    def key_pieces(rows):
        return jnp.repeat(pieces(rows, HEAD_FEATURES), copies, axis=0)

    kv_send = jnp.stack([key_pieces(keys), key_pieces(values)], axis=1)
    kv = lax.all_to_all(kv_send, "uly", 0, 0, tiled=True)
    qd_send = jnp.stack([pieces(queries, width), pieces(grad_out, width)], axis=1)
    qd = lax.all_to_all(qd_send, "uly", 0, 0, tiled=True)
    slots = lax.all_to_all(kv[send_block], "blk", 0, 0, tiled=True)

    def stat_rows(stat):
        return (
            stat.reshape(block_count, BLOCK, local_heads)
            .transpose(0, 2, 1)
            .reshape(block_count, 1, width)
        )

    stats = jnp.concatenate([stat_rows(row_lse), stat_rows(row_delta)], axis=1)
    grad_q, acc, memory_dk, memory_dv = attention(
        pair_index, pair_far, qd, kv, slots, stats, memory_keys, memory_values
    )
    back = acc[:, block_count:].transpose(1, 0, 2, 3).astype(jnp.bfloat16)
    back = lax.all_to_all(back, "blk", 0, 0, tiled=True)
    chosen = jax.nn.one_hot(send_block, block_count, dtype=jnp.float32)
    total = acc[:, :block_count].transpose(1, 0, 2, 3)
    total = total + jnp.einsum(
        "sb,strd->btrd", chosen, back.astype(jnp.float32), precision=lax.Precision.HIGHEST
    )
    scale = jnp.array([SCALE, 1.0], jnp.float32)[None, :, None, None]
    total = (total * scale).astype(jnp.bfloat16)
    grad_q = lax.all_to_all(grad_q, "uly", 0, 0, tiled=True)
    grad_kv = lax.all_to_all(total, "uly", 0, 0, tiled=True)
    grad_kv = jnp.sum(
        grad_kv.astype(jnp.float32).reshape(KEY_HEADS, copies, 2, present_rows, HEAD_FEATURES),
        axis=1,
    )
    grad_k = grad_kv[:, 0].transpose(1, 0, 2).reshape(present_rows, KEY_HEADS * HEAD_FEATURES)
    grad_v = grad_kv[:, 1].transpose(1, 0, 2).reshape(present_rows, KEY_HEADS * HEAD_FEATURES)
    grad_q = grad_q.transpose(1, 0, 2).reshape(present_rows, QUERY_HEADS * HEAD_FEATURES)
    memory_dk, memory_dv = lax.psum((memory_dk, memory_dv), "blk")
    return grad_q, grad_k, grad_v, memory_dk, memory_dv


def solution(mesh):
    in_specs = (
        P(("blk", "uly"), None),
        P(("blk", "uly"), None),
        P(("blk", "uly"), None),
        P(("blk", "uly"), None),
        P("blk", "uly"),
        P("blk", "uly"),
        P(),
        P(None, "uly"),
        P(None, "uly"),
    )
    out_specs = (
        P(("blk", "uly"), None),
        P(("blk", "uly"), None),
        P(("blk", "uly"), None),
        P(None, "uly"),
        P(None, "uly"),
    )
    return jax.shard_map(shards, mesh=mesh, in_specs=in_specs, out_specs=out_specs, check_vma=False)
```

```python
import functools
import math

import jax
import jax.numpy as jnp
from jax import lax
from jax.experimental import pallas as pl
from jax.experimental.pallas import tpu as pltpu
from jax.sharding import PartitionSpec as P

QUERY_HEADS = 32
KEY_HEADS = 8
HEAD_FEATURES = 128
BLOCK = 128
RANDOM = 2
SEQ_PAIRS = RANDOM + 3
GROUP = QUERY_HEADS // KEY_HEADS
SCALE = HEAD_FEATURES ** (-0.5)
LOG2E = math.log2(math.e)
FAR = 1e30
MAX_PERMUTES = 8
VMEM_LIMIT = 24 * 1024 * 1024
NN = (((1,), (0,)), ((), ()))
NT = (((1,), (1,)), ((), ()))
SMEM_SPEC = pl.BlockSpec(memory_space=pltpu.SMEM)
VMEM_SPEC = pl.BlockSpec(memory_space=pltpu.VMEM)


def dot(left, right, dims=NN):
    return lax.dot_general(left, right, dims, preferred_element_type=jnp.float32)


def col(at, width=HEAD_FEATURES):
    if isinstance(at, int):
        return pl.ds(at * width, width)
    return pl.ds(pl.multiple_of(at * width, width), width)


def even(n):
    return n & (n - 1) == 0


def partner(me, k, n):
    return me ^ k if even(n) else lax.rem(k - me + n, n)


def skipped(k, n):
    return even(n) and k == 0


def exchange(pieces, axis):
    n = lax.axis_size(axis)
    if even(n) and n <= MAX_PERMUTES:
        return [pieces[0]] + [
            lax.ppermute(pieces[k], axis, [(i, i ^ k) for i in range(n)]) for k in range(1, n)
        ]
    order = partner(lax.axis_index(axis), jnp.arange(n, dtype=jnp.int32), n)
    sent = jnp.stack(pieces)[order]
    return list(lax.all_to_all(sent, axis, 0, 0, tiled=True)[order])


def call(kernel, outs, ctl, *operands, scratch=(), flops=0, trans=0):
    moved = sum(math.prod(x.shape) * x.dtype.itemsize for x in [*operands, *outs])
    return pl.pallas_call(
        kernel,
        in_specs=[SMEM_SPEC] + [VMEM_SPEC] * len(operands),
        out_specs=[VMEM_SPEC] * len(outs),
        out_shape=[jax.ShapeDtypeStruct(x.shape, x.dtype) for x in outs],
        scratch_shapes=list(scratch),
        compiler_params=pltpu.CompilerParams(vmem_limit_bytes=VMEM_LIMIT),
        cost_estimate=pl.CostEstimate(flops=flops, bytes_accessed=moved, transcendentals=trans),
    )(ctl, *operands)


def array(shape, dtype=jnp.bfloat16):
    return jax.ShapeDtypeStruct(shape, dtype)


class Layout:
    def __init__(self, ways, spans):
        self.ways = ways
        self.spans = spans
        self.heads = QUERY_HEADS // ways
        self.width = self.heads * HEAD_FEATURES
        self.mem_rows = BLOCK // spans if BLOCK % spans == 0 else 0

    def key_head(self, device):
        return lax.div(device * self.heads, GROUP)

    def pool_index(self, ctl, block):
        me, span = ctl[0], ctl[1]
        owner = lax.div(block, self.ways)
        local = lax.rem(block, self.ways)
        mine = partner(me, local, self.ways)
        slot = self.ways + partner(span, owner, self.spans)
        return jnp.where(owner == span, mine, slot)

    def pairs(self, ctl, k):
        me, span = ctl[0], ctl[1]
        block = span * self.ways + partner(me, k, self.ways)
        last = self.ways * self.spans - 1
        index = [
            self.pool_index(ctl, jnp.maximum(block - 1, 0)),
            self.pool_index(ctl, block),
            self.pool_index(ctl, jnp.minimum(block + 1, last)),
        ]
        index += [self.pool_index(ctl, ctl[2 + block * RANDOM + r]) for r in range(RANDOM)]
        far = [jnp.where(block == 0, FAR, 0.0), 0.0, jnp.where(block == last, FAR, 0.0)]
        return index, far + [0.0] * RANDOM

    def send_index(self, ctl, k):
        me, span = ctl[0], ctl[1]
        other = partner(span, k, self.spans)
        entries = self.ways * RANDOM

        def look(e, found):
            block = ctl[2 + other * entries + e]
            return jnp.where(lax.div(block, self.ways) == span, lax.rem(block, self.ways), found)

        named = lax.fori_loop(0, entries, look, jnp.int32(0))
        local = jnp.where(
            other == span + 1, self.ways - 1, jnp.where(other == span - 1, 0, named)
        )
        return partner(me, local, self.ways)


def cut_kernel(lay, column, ctl, *refs):
    first, second, *pieces = refs
    for k, piece in enumerate(pieces):
        at = col(column(partner(ctl[0], k, lay.ways)), piece.shape[2])
        piece[0] = first[:, at]
        piece[1] = second[:, at]


def cut(lay, column, ctl, first, second, width):
    return call(
        functools.partial(cut_kernel, lay, column),
        [array((2, BLOCK, width))] * lay.ways,
        ctl,
        first,
        second,
    )


def pool_kernel(lay, ctl, *refs):
    pieces = refs[: lay.ways]
    pool, *slots = refs[lay.ways :]
    for k, piece in enumerate(pieces):
        pool[k, 0] = piece[0]
        pool[k, 1] = piece[1]
        pool[k, 2] = piece[0].T
    for k, slot in enumerate(slots):
        if not skipped(k, lay.spans):
            at = lay.send_index(ctl, k)
            slot[0] = pool[at, 0]
            slot[1] = pool[at, 1]
        else:
            slot[...] = pieces[0][...]


def attention_kernel(lay, ks, first, last, ctl, *refs):
    refs = list(refs)
    take = lambda n: [refs.pop(0) for _ in range(n)]
    looped = len(ks) > MAX_PERMUTES // 2
    qds = take(1 if looped else len(ks))
    (pool,) = take(1)
    slots = take(lay.spans)
    stats, mk, mv = take(3)
    if not first:
        prev = take(3)
    dqs = take(1 if looped else len(ks))
    if last:
        local, own_mem = take(2)
        backs = take(lay.spans)
        acc, dmk, dmv, slot_pool, mkt = take(5)
    else:
        acc, dmk, dmv = take(3)
        slot_pool, mkt = take(2)
    heads = range(lay.heads)
    ways = lay.ways
    if first:
        for total in (acc, dmk, dmv):
            total[...] = jnp.zeros_like(total)
    else:
        for total, before in zip((acc, dmk, dmv), prev):
            total[...] = before[...]
    slot_pool[:ways] = pool[...]
    for s, slot in enumerate(slots):
        slot_pool[ways + s, 0] = slot[0]
        slot_pool[ways + s, 1] = slot[1]
        slot_pool[ways + s, 2] = slot[0].T
    for h in heads:
        mkt[h] = mk[:, col(h)].T

    def one_block(k, qd, dq):
        index, far = lay.pairs(ctl, k)
        stat = stats[partner(ctl[0], k, ways)]
        lse = jnp.concatenate([stat[h : h + 1] for h in heads], axis=1) * LOG2E
        delta = jnp.concatenate([stat[lay.heads + h : lay.heads + h + 1] for h in heads], axis=1)
        q_heads = [qd[0, :, col(h)] for h in heads]
        do_heads = [qd[1, :, col(h)] for h in heads]
        q_all = jnp.concatenate(q_heads, axis=0)
        do_all = jnp.concatenate(do_heads, axis=0)
        keys = jnp.concatenate([slot_pool[i, 0] for i in index], axis=0)
        values = jnp.concatenate([slot_pool[i, 1] for i in index], axis=0)
        keys_t = jnp.concatenate([slot_pool[i, 2] for i in index], axis=1)

        def weigh(scores, dweights, lse_row):
            weights = jnp.exp2(scores * (SCALE * LOG2E) - lse_row)
            dscores = weights * (dweights - delta)
            return weights.astype(jnp.bfloat16), dscores.astype(jnp.bfloat16)

        scores = dot(keys, q_all, NT)
        dweights = dot(values, do_all, NT)
        parts = []
        for j in range(SEQ_PAIRS):
            rows = slice(j * BLOCK, (j + 1) * BLOCK)
            parts.append(weigh(scores[rows], dweights[rows], lse + far[j]))
        weights = jnp.concatenate([w for w, _ in parts], axis=0)
        dscores = jnp.concatenate([d for _, d in parts], axis=0)
        dq_t = dot(keys_t, dscores)
        dk = dot(dscores, q_all)
        dv = dot(weights, do_all)
        for j, i in enumerate(index):
            rows = slice(j * BLOCK, (j + 1) * BLOCK)
            acc[i, 0] += dk[rows]
            acc[i, 1] += dv[rows]

        mem_scores = jnp.concatenate([dot(mk[:, col(h)], q_heads[h], NT) for h in heads], axis=1)
        mem_dweights = jnp.concatenate(
            [dot(mv[:, col(h)], do_heads[h], NT) for h in heads], axis=1
        )
        mem_w, mem_d = weigh(mem_scores, mem_dweights, lse)
        for h in heads:
            lanes = slice(h * HEAD_FEATURES, (h + 1) * HEAD_FEATURES)
            dmk[:, col(h)] += dot(mem_d[:, lanes], q_heads[h])
            dmv[:, col(h)] += dot(mem_w[:, lanes], do_heads[h])
            head_dq = dq_t[:, lanes] + dot(mkt[h], mem_d[:, lanes])
            dq[:, col(h)] = (head_dq * SCALE).T.astype(jnp.bfloat16)

    if looped:

        @pl.loop(0, len(ks))
        def _(i):
            one_block(ks[0] + i, qds[0].at[i], dqs[0].at[i])
    else:
        for k, qd, dq in zip(ks, qds, dqs):
            one_block(k, qd, dq)

    if last:
        local[...] = acc[:ways]
        for s, back in enumerate(backs):
            back[0] = (acc[ways + s, 0] * SCALE).astype(jnp.bfloat16)
            back[1] = acc[ways + s, 1].astype(jnp.bfloat16)
            if lay.mem_rows:
                rows = mem_part(lay, ctl, s)
                for h in heads:
                    at = pl.ds(h * lay.mem_rows, lay.mem_rows)
                    back[2, at] = (dmk[rows, col(h)] * SCALE).astype(jnp.bfloat16)
                    back[3, at] = dmv[rows, col(h)].astype(jnp.bfloat16)
        if lay.mem_rows:
            rows = mem_part(lay, ctl, 0)
            own_mem[0] = dmk[rows] * SCALE
            own_mem[1] = dmv[rows]
        else:
            own_mem[0] = dmk[...] * SCALE
            own_mem[1] = dmv[...]


def mem_part(lay, ctl, k):
    at = partner(ctl[1], k, lay.spans) * lay.mem_rows
    return pl.ds(pl.multiple_of(at, lay.mem_rows), lay.mem_rows)


def attention(lay, ks, ctl, qds, pool, slots, stats, mk, mv, before, last):
    blocks = lay.ways + lay.spans
    totals = [
        array((blocks, 2, BLOCK, HEAD_FEATURES), jnp.float32),
        array((BLOCK, lay.width), jnp.float32),
        array((BLOCK, lay.width), jnp.float32),
    ]
    scratch = [
        pltpu.VMEM((blocks, 3, BLOCK, HEAD_FEATURES), jnp.bfloat16),
        pltpu.VMEM((lay.heads, BLOCK, HEAD_FEATURES), jnp.bfloat16),
    ]
    pieces = [qds[k] for k in ks]
    outs = [array((BLOCK, lay.width))] * len(ks)
    looped = len(ks) > MAX_PERMUTES // 2
    if looped:
        pieces = [jnp.stack(pieces)]
        outs = [array((len(ks), BLOCK, lay.width))]
    if last:
        outs += [
            array((lay.ways, 2, BLOCK, HEAD_FEATURES), jnp.float32),
            array((2, lay.mem_rows or BLOCK, lay.width), jnp.float32),
        ]
        outs += [array((4 if lay.mem_rows else 2, BLOCK, HEAD_FEATURES))] * lay.spans
        scratch = [pltpu.VMEM(t.shape, t.dtype) for t in totals] + scratch
    else:
        outs += totals
    pairs = len(ks) * lay.heads * (SEQ_PAIRS + 1)
    done = call(
        functools.partial(attention_kernel, lay, ks, before is None, last),
        outs,
        ctl,
        *pieces,
        pool,
        *slots,
        stats,
        mk,
        mv,
        *(before or []),
        scratch=scratch,
        flops=pairs * 10 * BLOCK * BLOCK * HEAD_FEATURES,
        trans=pairs * BLOCK * BLOCK,
    )
    return [*done[0], *done[1:]] if looped else done


def merge_kernel(lay, ctl, *refs):
    local, own_mem = refs[:2]
    backs = refs[2 : 2 + lay.spans]
    pieces = refs[2 + lay.spans : 2 + lay.spans + lay.ways]
    mem_sum, total = refs[2 + lay.spans + lay.ways :]
    for k in range(lay.ways):
        total[k, 0] = local[k, 0] * SCALE
        total[k, 1] = local[k, 1]
    mem_sum[...] = own_mem[...]
    for s, back in enumerate(backs):
        if skipped(s, lay.spans):
            continue
        at = lay.send_index(ctl, s)
        for i in range(2):
            total[at, i] += back[i].astype(jnp.float32)
            for h in range(lay.heads if lay.mem_rows else 0):
                rows = pl.ds(h * lay.mem_rows, lay.mem_rows)
                mem_sum[i, :, col(h)] += back[2 + i, rows].astype(jnp.float32)
    for k, piece in enumerate(pieces):
        piece[...] = total[k].astype(jnp.bfloat16)


def join_kernel(lay, ctl, *refs):
    *pieces, out = refs
    for k, piece in enumerate(pieces):
        out[:, col(partner(ctl[0], k, lay.ways), lay.width)] = piece[...]


def finish_kernel(lay, ctl, *refs):
    pieces = refs[: lay.ways]
    parts = refs[lay.ways : -4]
    out_k, out_v, out_mk, out_mv = refs[-4:]
    shared = lay.heads < GROUP
    if shared:
        out_k[...] = jnp.zeros_like(out_k)
        out_v[...] = jnp.zeros_like(out_v)
    for k, piece in enumerate(pieces):
        at = col(lay.key_head(partner(ctl[0], k, lay.ways)))
        for i, out in enumerate((out_k, out_v)):
            term = piece[i].astype(jnp.float32)
            out[:, at] = out[:, at] + term if shared else term
    for s, part in enumerate(parts):
        rows = mem_part(lay, ctl, s) if lay.mem_rows else slice(None)
        out_mk[rows, :] = part[0]
        out_mv[rows, :] = part[1]


def shards(
    queries, keys, values, grad_out, row_lse, row_delta, pattern, memory_keys, memory_values
):
    lay = Layout(lax.axis_size("uly"), lax.axis_size("blk"))
    place = jnp.stack([lax.axis_index("uly"), lax.axis_index("blk")]).astype(jnp.int32)
    ctl = jnp.concatenate([place, pattern.reshape(-1)])

    kv = exchange(cut(lay, lay.key_head, ctl, keys, values, HEAD_FEATURES), "uly")
    qd = exchange(cut(lay, lambda device: device, ctl, queries, grad_out, lay.width), "uly")
    stats = jnp.concatenate([row_lse, row_delta], axis=1)
    stats = stats.reshape(lay.ways, BLOCK, 2 * lay.heads).transpose(0, 2, 1)

    pool, *slots = call(
        functools.partial(pool_kernel, lay),
        [array((lay.ways, 3, BLOCK, HEAD_FEATURES))]
        + [array((2, BLOCK, HEAD_FEATURES))] * lay.spans,
        ctl,
        *kv,
    )
    slots = exchange(slots, "blk")

    half = max(1, lay.ways // 4)
    steps = [range(0, 2 * half), range(2 * half, 3 * half), range(3 * half, lay.ways)]
    totals, dq = None, []
    for step in steps:
        last = step is steps[-1]
        ks = list(step)
        done = attention(
            lay, ks, ctl, qd, pool, slots, stats, memory_keys, memory_values, totals, last
        )
        dq += done[: len(ks)]
        totals = done[len(ks) :]
    local, own_mem, *backs = totals
    backs = exchange(backs, "blk")
    dq = exchange(dq, "uly")
    *dkv, mem = call(
        functools.partial(merge_kernel, lay),
        [array((2, BLOCK, HEAD_FEATURES))] * lay.ways + [array(own_mem.shape, jnp.float32)],
        ctl,
        local,
        own_mem,
        *backs,
        scratch=[pltpu.VMEM((lay.ways, 2, BLOCK, HEAD_FEATURES), jnp.float32)],
    )
    dkv = exchange(dkv, "uly")
    mem = exchange([mem] * lay.spans, "blk") if lay.mem_rows else [lax.psum(mem, "blk")]
    (grad_q,) = call(
        functools.partial(join_kernel, lay),
        [array(queries.shape)],
        ctl,
        *dq,
    )
    grad_k, grad_v, grad_mk, grad_mv = call(
        functools.partial(finish_kernel, lay),
        [array(keys.shape, jnp.float32)] * 2 + [array(memory_keys.shape, jnp.float32)] * 2,
        ctl,
        *dkv,
        *mem,
    )
    return grad_q, grad_k, grad_v, grad_mk, grad_mv


def solution(mesh):
    in_specs = (
        P(("blk", "uly"), None),
        P(("blk", "uly"), None),
        P(("blk", "uly"), None),
        P(("blk", "uly"), None),
        P("blk", "uly"),
        P("blk", "uly"),
        P(),
        P(None, "uly"),
        P(None, "uly"),
    )
    out_specs = (
        P(("blk", "uly"), None),
        P(("blk", "uly"), None),
        P(("blk", "uly"), None),
        P(None, "uly"),
        P(None, "uly"),
    )
    return jax.shard_map(shards, mesh=mesh, in_specs=in_specs, out_specs=out_specs, check_vma=False)
```

```python
import functools
import math

import jax
import jax.numpy as jnp
from jax import lax
from jax.experimental import pallas as pl
from jax.experimental.pallas import tpu as pltpu
from jax.sharding import PartitionSpec as P

QUERY_HEADS = 32
KEY_HEADS = 8
HEAD_FEATURES = 128
BLOCK = 128
RANDOM = 2
SEQ_PAIRS = RANDOM + 3
GROUP = QUERY_HEADS // KEY_HEADS
SCALE = HEAD_FEATURES ** (-0.5)
LOG2E = math.log2(math.e)
FAR = 1e30
MAX_PERMUTES = 8
VMEM_LIMIT = 24 * 1024 * 1024
WIDE_LIMIT = 60 * 1024 * 1024
NN = (((1,), (0,)), ((), ()))
NT = (((1,), (1,)), ((), ()))
SMEM_SPEC = pl.BlockSpec(memory_space=pltpu.SMEM)


def dot(left, right, dims=NN):
    return lax.dot_general(left, right, dims, preferred_element_type=jnp.float32)


def col(at, width=HEAD_FEATURES):
    if isinstance(at, int):
        return pl.ds(at * width, width)
    return pl.ds(pl.multiple_of(at * width, width), width)


def even(n):
    return n & (n - 1) == 0


def partner(me, k, n):
    return me ^ k if even(n) else lax.rem(k - me + n, n)


def staged(n):
    return even(n) and n <= MAX_PERMUTES


def swap(piece, k):
    return lax.ppermute(piece, "uly", [(i, i ^ k) for i in range(lax.axis_size("uly"))])


def to_spans(stacked):
    return lax.all_to_all(stacked, "blk", 0, 0, tiled=True)


def after(early, late):
    early, late = lax.optimization_barrier((early, late))
    return early, late


def call(kernel, outs, ctl, *operands, scratch=(), limit=VMEM_LIMIT):
    outputs = pl.pallas_call(
        kernel,
        in_specs=[SMEM_SPEC] + [pl.BlockSpec(memory_space=pltpu.VMEM)] * len(operands),
        out_specs=[pl.BlockSpec(memory_space=pltpu.VMEM)] * len(outs),
        out_shape=[jax.ShapeDtypeStruct(x.shape, x.dtype) for x in outs],
        scratch_shapes=list(scratch),
        compiler_params=pltpu.CompilerParams(vmem_limit_bytes=limit),
        cost_estimate=pl.CostEstimate(flops=0, bytes_accessed=0, transcendentals=0),
    )(ctl, *operands)
    return list(outputs)


def array(shape, dtype=jnp.bfloat16):
    return jax.ShapeDtypeStruct(shape, dtype)


class Layout:
    def __init__(self, ways, spans):
        self.ways = ways
        self.spans = spans
        self.heads = QUERY_HEADS // ways
        self.width = self.heads * HEAD_FEATURES
        self.mem_rows = BLOCK // spans if BLOCK % spans == 0 else 0

    def key_head(self, device):
        return lax.div(device * self.heads, GROUP)

    def pool_index(self, ctl, block):
        me, span = ctl[0], ctl[1]
        owner = lax.div(block, self.ways)
        local = lax.rem(block, self.ways)
        mine = partner(me, local, self.ways)
        return jnp.where(owner == span, mine, self.ways + owner)

    def pairs(self, ctl, k):
        me, span = ctl[0], ctl[1]
        block = span * self.ways + partner(me, k, self.ways)
        last = self.ways * self.spans - 1
        index = [
            self.pool_index(ctl, jnp.maximum(block - 1, 0)),
            self.pool_index(ctl, block),
            self.pool_index(ctl, jnp.minimum(block + 1, last)),
        ]
        index += [self.pool_index(ctl, ctl[2 + block * RANDOM + r]) for r in range(RANDOM)]
        far = [jnp.where(block == 0, FAR, 0.0), 0.0, jnp.where(block == last, FAR, 0.0)]
        return index, far + [0.0] * RANDOM

    def send_index(self, ctl, other):
        me, span = ctl[0], ctl[1]
        entries = self.ways * RANDOM

        def look(e, found):
            block = ctl[2 + other * entries + e]
            return jnp.where(lax.div(block, self.ways) == span, lax.rem(block, self.ways), found)

        named = lax.fori_loop(0, entries, look, jnp.int32(0))
        local = jnp.where(
            other == span + 1, self.ways - 1, jnp.where(other == span - 1, 0, named)
        )
        return partner(me, local, self.ways)


def cut_kernel(column, ks, ctl, first, second, out):
    for n, k in enumerate(ks):
        at = col(column(partner(ctl[0], k, lax.axis_size("uly"))), out.shape[3])
        out[n, 0] = first[:, at]
        out[n, 1] = second[:, at]


def cut(column, ks, ctl, first, second, width):
    out = array((len(ks), 2, BLOCK, width))
    return call(functools.partial(cut_kernel, column, ks), [out], ctl, first, second)[0]


def pack_kernel(column, ctl, first, second, got, *outs):
    for j, out in enumerate(outs):
        at = col(column(partner(ctl[0], 2 * j, lax.axis_size("uly"))), out.shape[3])
        out[0, 0] = first[:, at]
        out[0, 1] = second[:, at]
        out[1] = got[j]


def by_chip(column, ctl, first, second, width):
    ways = lax.axis_size("uly")
    chips = ways // 2
    if staged(ways):
        got = swap(cut(column, range(1, ways, 2), ctl, first, second, width), 1)
        return call(
            functools.partial(pack_kernel, column),
            [array((2, 2, BLOCK, width))] * chips,
            ctl,
            first,
            second,
            got,
        )
    order = partner(lax.axis_index("uly"), jnp.arange(ways, dtype=jnp.int32), ways)
    sent = cut(column, range(ways), ctl, first, second, width)[order]
    got = lax.all_to_all(sent, "uly", 0, 0, tiled=True)[order]
    return list(got.reshape(chips, 2, 2, BLOCK, width))


def pick_kernel(ctl, *refs):
    *pieces, out = refs
    for j, piece in enumerate(pieces):
        out[j] = piece[1]


def to_blocks(pieces):
    out = array((len(pieces), *pieces[0].shape[1:]), pieces[0].dtype)
    (other,) = call(pick_kernel, [out], jnp.zeros((1,), jnp.int32), *pieces)
    return swap(other, 1)


def pool_kernel(lay, ctl, *refs):
    *pieces, pool, slots = refs
    for j, piece in enumerate(pieces):
        for i in range(2):
            pool[2 * j + i, 0] = piece[i, 0]
            pool[2 * j + i, 1] = piece[i, 1]
            pool[2 * j + i, 2] = piece[i, 0].T
    for s in range(lay.spans):
        at = lay.send_index(ctl, s)
        slots[s, 0] = pool[at, 0]
        slots[s, 1] = pool[at, 1]


def attention_kernel(lay, js, first, last, ctl, *refs):
    refs = list(refs)
    take = lambda n: [refs.pop(0) for _ in range(n)]
    looped = len(js) > MAX_PERMUTES // 2
    qds = take(1 if looped else len(js))
    pool, slots, stats, mk, mv = take(5)
    if not first:
        prev = take(3)
    dqs = take(1 if looped else len(js))
    if last:
        local, own_mem, backs = take(3)
        acc, dmk, dmv, slot_pool, mkt = take(5)
    else:
        acc, dmk, dmv = take(3)
        slot_pool, mkt = take(2)
    heads = range(lay.heads)
    ways = lay.ways
    if first:
        for total in (acc, dmk, dmv):
            total[...] = jnp.zeros_like(total)
    else:
        for total, before in zip((acc, dmk, dmv), prev):
            total[...] = before[...]
    slot_pool[:ways] = pool[...]
    for s in range(lay.spans):
        slot_pool[ways + s, 0] = slots[s, 0]
        slot_pool[ways + s, 1] = slots[s, 1]
        slot_pool[ways + s, 2] = slots[s, 0].T
    for h in heads:
        mkt[h] = mk[:, col(h)].T

    def one_block(k, qd, dq):
        index, far = lay.pairs(ctl, k)
        stat = stats[partner(ctl[0], k, ways)]
        lse = jnp.concatenate([stat[h : h + 1] for h in heads], axis=1) * LOG2E
        delta = jnp.concatenate([stat[lay.heads + h : lay.heads + h + 1] for h in heads], axis=1)
        q_heads = [qd[0, :, col(h)] for h in heads]
        do_heads = [qd[1, :, col(h)] for h in heads]
        q_all = jnp.concatenate(q_heads, axis=0)
        do_all = jnp.concatenate(do_heads, axis=0)
        keys = jnp.concatenate([slot_pool[i, 0] for i in index], axis=0)
        values = jnp.concatenate([slot_pool[i, 1] for i in index], axis=0)
        keys_t = jnp.concatenate([slot_pool[i, 2] for i in index], axis=1)

        def weigh(scores, dweights, lse_row):
            weights = jnp.exp2(scores * (SCALE * LOG2E) - lse_row)
            dscores = weights * (dweights - delta)
            return weights.astype(jnp.bfloat16), dscores.astype(jnp.bfloat16)

        scores = dot(keys, q_all, NT)
        dweights = dot(values, do_all, NT)
        parts = []
        for j in range(SEQ_PAIRS):
            rows = slice(j * BLOCK, (j + 1) * BLOCK)
            parts.append(weigh(scores[rows], dweights[rows], lse + far[j]))
        weights = jnp.concatenate([w for w, _ in parts], axis=0)
        dscores = jnp.concatenate([d for _, d in parts], axis=0)
        dq_t = dot(keys_t, dscores)
        dk = dot(dscores, q_all)
        dv = dot(weights, do_all)
        for j, i in enumerate(index):
            rows = slice(j * BLOCK, (j + 1) * BLOCK)
            acc[i, 0] += dk[rows]
            acc[i, 1] += dv[rows]

        mem_scores = jnp.concatenate([dot(mk[:, col(h)], q_heads[h], NT) for h in heads], axis=1)
        mem_dweights = jnp.concatenate(
            [dot(mv[:, col(h)], do_heads[h], NT) for h in heads], axis=1
        )
        mem_w, mem_d = weigh(mem_scores, mem_dweights, lse)
        for h in heads:
            lanes = slice(h * HEAD_FEATURES, (h + 1) * HEAD_FEATURES)
            dmk[:, col(h)] += dot(mem_d[:, lanes], q_heads[h])
            dmv[:, col(h)] += dot(mem_w[:, lanes], do_heads[h])
            head_dq = dq_t[:, lanes] + dot(mkt[h], mem_d[:, lanes])
            dq[:, col(h)] = (head_dq * SCALE).T.astype(jnp.bfloat16)

    if looped:

        @pl.loop(0, len(js))
        def _(n):
            for i in range(2):
                one_block(2 * (js[0] + n) + i, qds[0].at[n, i], dqs[0].at[n, i])
    else:
        for j, qd, dq in zip(js, qds, dqs):
            for i in range(2):
                one_block(2 * j + i, qd.at[i], dq.at[i])

    if last:
        local[...] = acc[:ways]
        for s in range(lay.spans):
            backs[s, 0] = (acc[ways + s, 0] * SCALE).astype(jnp.bfloat16)
            backs[s, 1] = acc[ways + s, 1].astype(jnp.bfloat16)
            for h in heads if lay.mem_rows else ():
                rows = pl.ds(s * lay.mem_rows, lay.mem_rows)
                at = pl.ds(h * lay.mem_rows, lay.mem_rows)
                backs[s, 2, at] = (dmk[rows, col(h)] * SCALE).astype(jnp.bfloat16)
                backs[s, 3, at] = dmv[rows, col(h)].astype(jnp.bfloat16)
        rows = slice(None)
        if lay.mem_rows:
            rows = pl.ds(pl.multiple_of(ctl[1] * lay.mem_rows, lay.mem_rows), lay.mem_rows)
        own_mem[0] = dmk[rows, :] * SCALE
        own_mem[1] = dmv[rows, :]


def attention(lay, js, ctl, qds, pool, slots, stats, mk, mv, before, last):
    blocks = lay.ways + lay.spans
    totals = [
        array((blocks, 2, BLOCK, HEAD_FEATURES), jnp.float32),
        array((BLOCK, lay.width), jnp.float32),
        array((BLOCK, lay.width), jnp.float32),
    ]
    scratch = [
        pltpu.VMEM((blocks, 3, BLOCK, HEAD_FEATURES), jnp.bfloat16),
        pltpu.VMEM((lay.heads, BLOCK, HEAD_FEATURES), jnp.bfloat16),
    ]
    pieces = [qds[j] for j in js]
    outs = [array((2, BLOCK, lay.width))] * len(js)
    looped = len(js) > MAX_PERMUTES // 2
    if looped:
        pieces = [jnp.stack(pieces)]
        outs = [array((len(js), 2, BLOCK, lay.width))]
    if last:
        outs += [
            array((lay.ways, 2, BLOCK, HEAD_FEATURES), jnp.float32),
            array((2, lay.mem_rows or BLOCK, lay.width), jnp.float32),
            array((lay.spans, 4 if lay.mem_rows else 2, BLOCK, HEAD_FEATURES)),
        ]
        scratch = [pltpu.VMEM(t.shape, t.dtype) for t in totals] + scratch
    else:
        outs += totals
    done = call(
        functools.partial(attention_kernel, lay, js, before is None, last),
        outs,
        ctl,
        *pieces,
        pool,
        slots,
        stats,
        mk,
        mv,
        *(before or []),
        scratch=scratch,
    )
    dq = done[0] if looped else done[: len(js)]
    return dict(zip(js, dq)), done[1 if looped else len(js) :]


def merge_kernel(lay, ctl, local, own_mem, backs, *refs):
    *pieces, mem_sum, total = refs
    for k in range(lay.ways):
        total[k, 0] = local[k, 0] * SCALE
        total[k, 1] = local[k, 1]
    mem = [own_mem[0], own_mem[1]]
    for s in range(lay.spans):

        @pl.when(s != ctl[1])
        def _():
            at = lay.send_index(ctl, s)
            for i in range(2):
                total[at, i] += backs[s, i].astype(jnp.float32)

        if lay.mem_rows:
            for i in range(2):
                term = [
                    backs[s, 2 + i, pl.ds(h * lay.mem_rows, lay.mem_rows)]
                    for h in range(lay.heads)
                ]
                term = jnp.concatenate(term, axis=1).astype(jnp.float32)
                mem[i] += jnp.where(s == ctl[1], 0.0, term)
    for s in range(mem_sum.shape[0]):
        for i in range(2):
            mem_sum[s, i] = mem[i]
    for j, piece in enumerate(pieces):
        for i in range(2):
            piece[i] = total[2 * j + i].astype(jnp.bfloat16)


def by_partner(refs):
    *pieces, others = refs
    for j, piece in enumerate(pieces):
        yield 2 * j, piece.at[0]
        yield 2 * j + 1, others.at[j]


def join_kernel(lay, ctl, *refs):
    *pieces, out = refs
    for k, piece in by_partner(pieces):
        out[:, col(partner(ctl[0], k, lay.ways), lay.width)] = piece[...]


def finish_kernel(lay, ctl, mem, *refs):
    *pieces, out_k, out_v, out_mk, out_mv = refs
    shared = lay.heads < GROUP
    if shared:
        out_k[...] = jnp.zeros_like(out_k)
        out_v[...] = jnp.zeros_like(out_v)
    for k, piece in by_partner(pieces):
        at = col(lay.key_head(partner(ctl[0], k, lay.ways)))
        for i, out in enumerate((out_k, out_v)):
            term = piece[i].astype(jnp.float32)
            out[:, at] = out[:, at] + term if shared else term
    for s in range(mem.shape[0]):
        rows = pl.ds(s * mem.shape[2], mem.shape[2])
        out_mk[rows, :] = mem[s, 0]
        out_mv[rows, :] = mem[s, 1]


def whole_exchange(pieces):
    ways = 2 * len(pieces)
    order = partner(lax.axis_index("uly"), jnp.arange(ways, dtype=jnp.int32), ways)
    sent = jnp.concatenate(pieces)[order]
    got = lax.all_to_all(sent, "uly", 0, 0, tiled=True)[order]
    got = got.reshape(len(pieces), 2, *got.shape[1:])
    return [*got, got[:, 1]]


def shards(
    queries, keys, values, grad_out, row_lse, row_delta, pattern, memory_keys, memory_values
):
    lay = Layout(lax.axis_size("uly"), lax.axis_size("blk"))
    chips = lay.ways // 2
    in_stages = staged(lay.ways)
    place = jnp.stack([lax.axis_index("uly"), lax.axis_index("blk")]).astype(jnp.int32)
    ctl = jnp.concatenate([place, pattern.reshape(-1)])

    qd = by_chip(lambda device: device, place, queries, grad_out, lay.width)
    late = place
    kv = by_chip(lay.key_head, late, keys, values, HEAD_FEATURES)
    steps = [range(chips)]
    if in_stages:
        half = max(1, chips // 2)
        steps = [range(half), *([j] for j in range(half, chips))]
        qd[half] = swap(qd[half], 2 * half)
        for j in [*range(half, chips), *range(1, half)]:
            kv[j] = swap(kv[j], 2 * j)
        kv[1:], qd[half + 1] = after(kv[1:], qd[half + 1])
        kv[1], qd[1] = after(kv[1], qd[1])
        qd[half + 1] = swap(qd[half + 1], 2 * half + 2)
        qd[1] = swap(qd[1], 2)
    pool, slots = call(
        functools.partial(pool_kernel, lay),
        [
            array((lay.ways, 3, BLOCK, HEAD_FEATURES)),
            array((lay.spans, 2, BLOCK, HEAD_FEATURES)),
        ],
        ctl,
        *kv,
    )
    slots = to_spans(slots)
    stats = jnp.concatenate([row_lse, row_delta], axis=1)
    stats = stats.reshape(lay.ways, BLOCK, 2 * lay.heads).transpose(0, 2, 1)

    totals, dq = None, {}
    for step in steps:
        last = step is steps[-1]
        step_dq, totals = attention(
            lay, step, ctl, qd, pool, slots, stats, memory_keys, memory_values, totals, last
        )
        dq |= step_dq
    local, own_mem, backs = totals
    backs = to_spans(backs)
    if in_stages:
        for j in [*range(half, chips), *range(1, half)]:
            dq[j] = swap(dq[j], 2 * j)
        pass
    *dkv, mem = call(
        functools.partial(merge_kernel, lay),
        [array((2, 2, BLOCK, HEAD_FEATURES))] * chips
        + [array((lay.spans if lay.mem_rows else 1, *own_mem.shape), jnp.float32)],
        ctl,
        local,
        own_mem,
        backs,
        scratch=[pltpu.VMEM((lay.ways, 2, BLOCK, HEAD_FEATURES), jnp.float32)],
    )
    mem = to_spans(mem) if lay.mem_rows else lax.psum(mem, "blk")
    dq = [dq[j] for j in range(chips)]
    if in_stages:
        for j in [*range(half, chips), *range(1, half)]:
            dkv[j] = swap(dkv[j], 2 * j)
        (dkv[1:], mem), dq = after((dkv[1:], mem), dq)
        dq.append(to_blocks(dq))
        dkv.append(to_blocks(dkv))
    else:
        dq = whole_exchange(dq)
        dkv = whole_exchange(dkv)
    (grad_q,) = call(functools.partial(join_kernel, lay), [array(queries.shape)], place, *dq)
    grad_k, grad_v, grad_mk, grad_mv = call(
        functools.partial(finish_kernel, lay),
        [array(keys.shape, jnp.float32)] * 2 + [array(memory_keys.shape, jnp.float32)] * 2,
        place,
        mem,
        *dkv,
    )
    return grad_q, grad_k, grad_v, grad_mk, grad_mv


def solution(mesh):
    in_specs = (
        P(("blk", "uly"), None),
        P(("blk", "uly"), None),
        P(("blk", "uly"), None),
        P(("blk", "uly"), None),
        P("blk", "uly"),
        P("blk", "uly"),
        P(),
        P(None, "uly"),
        P(None, "uly"),
    )
    out_specs = (
        P(("blk", "uly"), None),
        P(("blk", "uly"), None),
        P(("blk", "uly"), None),
        P(None, "uly"),
        P(None, "uly"),
    )
    return jax.shard_map(shards, mesh=mesh, in_specs=in_specs, out_specs=out_specs, check_vma=False)
```

```python
import functools
import math

import jax
import jax.numpy as jnp
from jax import lax
from jax.experimental import pallas as pl
from jax.experimental.pallas import tpu as pltpu
from jax.sharding import PartitionSpec as P

QUERY_HEADS = 32
KEY_HEADS = 8
HEAD_FEATURES = 128
BLOCK = 128
RANDOM = 2
SEQ_PAIRS = RANDOM + 3
GROUP = QUERY_HEADS // KEY_HEADS
SCALE = HEAD_FEATURES ** (-0.5)
LOG2E = math.log2(math.e)
FAR = 1e30
MAX_PERMUTES = 8
VMEM_LIMIT = 24 * 1024 * 1024
WIDE_LIMIT = 60 * 1024 * 1024
NN = (((1,), (0,)), ((), ()))
NT = (((1,), (1,)), ((), ()))
SMEM_SPEC = pl.BlockSpec(memory_space=pltpu.SMEM)


def dot(left, right, dims=NN):
    return lax.dot_general(left, right, dims, preferred_element_type=jnp.float32)


def col(at, width=HEAD_FEATURES):
    if isinstance(at, int):
        return pl.ds(at * width, width)
    return pl.ds(pl.multiple_of(at * width, width), width)


def even(n):
    return n & (n - 1) == 0


def partner(me, k, n):
    return me ^ k if even(n) else lax.rem(k - me + n, n)


def staged(n):
    return even(n) and n <= MAX_PERMUTES


def swap(piece, k):
    return lax.ppermute(piece, "uly", [(i, i ^ k) for i in range(lax.axis_size("uly"))])


def across_spans(pieces):
    spans = len(pieces)
    if even(spans) and spans <= MAX_PERMUTES:
        pairs = [[(i, i ^ k) for i in range(spans)] for k in range(spans)]
        return pieces[:1] + [lax.ppermute(pieces[k], "blk", pairs[k]) for k in range(1, spans)]
    order = partner(lax.axis_index("blk"), jnp.arange(spans, dtype=jnp.int32), spans)
    return list(to_spans(jnp.stack(pieces)[order])[order])


def to_spans(stacked):
    return lax.all_to_all(stacked, "blk", 0, 0, tiled=True)


def after(early, late):
    early, late = lax.optimization_barrier((early, late))
    return early, late


def call(kernel, outs, ctl, *operands, scratch=(), limit=VMEM_LIMIT):
    outputs = pl.pallas_call(
        kernel,
        in_specs=[SMEM_SPEC] + [pl.BlockSpec(memory_space=pltpu.VMEM)] * len(operands),
        out_specs=[pl.BlockSpec(memory_space=pltpu.VMEM)] * len(outs),
        out_shape=[jax.ShapeDtypeStruct(x.shape, x.dtype) for x in outs],
        scratch_shapes=list(scratch),
        compiler_params=pltpu.CompilerParams(vmem_limit_bytes=limit),
        cost_estimate=pl.CostEstimate(flops=0, bytes_accessed=0, transcendentals=0),
    )(ctl, *operands)
    return list(outputs)


def array(shape, dtype=jnp.bfloat16):
    return jax.ShapeDtypeStruct(shape, dtype)


class Layout:
    def __init__(self, ways, spans):
        self.ways = ways
        self.spans = spans
        self.heads = QUERY_HEADS // ways
        self.width = self.heads * HEAD_FEATURES
        self.mem_rows = BLOCK // spans if BLOCK % spans == 0 else 0

    def key_head(self, device):
        return lax.div(device * self.heads, GROUP)

    def pool_index(self, ctl, block):
        me, span = ctl[0], ctl[1]
        owner = lax.div(block, self.ways)
        local = lax.rem(block, self.ways)
        mine = partner(me, local, self.ways)
        return jnp.where(owner == span, mine, self.ways + owner)

    def pairs(self, ctl, k):
        me, span = ctl[0], ctl[1]
        block = span * self.ways + partner(me, k, self.ways)
        last = self.ways * self.spans - 1
        index = [
            self.pool_index(ctl, jnp.maximum(block - 1, 0)),
            self.pool_index(ctl, block),
            self.pool_index(ctl, jnp.minimum(block + 1, last)),
        ]
        index += [self.pool_index(ctl, ctl[2 + block * RANDOM + r]) for r in range(RANDOM)]
        far = [jnp.where(block == 0, FAR, 0.0), 0.0, jnp.where(block == last, FAR, 0.0)]
        return index, far + [0.0] * RANDOM

    def send_index(self, ctl, other):
        me, span = ctl[0], ctl[1]
        entries = self.ways * RANDOM

        def look(e, found):
            block = ctl[2 + other * entries + e]
            return jnp.where(lax.div(block, self.ways) == span, lax.rem(block, self.ways), found)

        named = lax.fori_loop(0, entries, look, jnp.int32(0))
        local = jnp.where(
            other == span + 1, self.ways - 1, jnp.where(other == span - 1, 0, named)
        )
        return partner(me, local, self.ways)


def cut_kernel(column, ks, ctl, first, second, out):
    for n, k in enumerate(ks):
        at = col(column(partner(ctl[0], k, lax.axis_size("uly"))), out.shape[3])
        out[n, 0] = first[:, at]
        out[n, 1] = second[:, at]


def cut(column, ks, ctl, first, second, width):
    out = array((len(ks), 2, BLOCK, width))
    return call(functools.partial(cut_kernel, column, ks), [out], ctl, first, second)[0]


def pack_kernel(column, ctl, first, second, got, *outs):
    for j, out in enumerate(outs):
        at = col(column(partner(ctl[0], 2 * j, lax.axis_size("uly"))), out.shape[3])
        out[0, 0] = first[:, at]
        out[0, 1] = second[:, at]
        out[1] = got[j]


def by_chip(column, ctl, first, second, width):
    ways = lax.axis_size("uly")
    chips = ways // 2
    if staged(ways):
        got = swap(cut(column, range(1, ways, 2), ctl, first, second, width), 1)
        return call(
            functools.partial(pack_kernel, column),
            [array((2, 2, BLOCK, width))] * chips,
            ctl,
            first,
            second,
            got,
        )
    order = partner(lax.axis_index("uly"), jnp.arange(ways, dtype=jnp.int32), ways)
    sent = cut(column, range(ways), ctl, first, second, width)[order]
    got = lax.all_to_all(sent, "uly", 0, 0, tiled=True)[order]
    return list(got.reshape(chips, 2, 2, BLOCK, width))


def pick_kernel(ctl, *refs):
    *pieces, out = refs
    for j, piece in enumerate(pieces):
        out[j] = piece[1]


def to_blocks(pieces):
    out = array((len(pieces), *pieces[0].shape[1:]), pieces[0].dtype)
    (other,) = call(pick_kernel, [out], jnp.zeros((1,), jnp.int32), *pieces)
    return swap(other, 1)


def pool_kernel(lay, ctl, *refs):
    *pieces, pool, slots = refs
    for j, piece in enumerate(pieces):
        for i in range(2):
            pool[2 * j + i, 0] = piece[i, 0]
            pool[2 * j + i, 1] = piece[i, 1]
            pool[2 * j + i, 2] = piece[i, 0].T
    for s in range(lay.spans):
        at = lay.send_index(ctl, s)
        slots[s, 0] = pool[at, 0]
        slots[s, 1] = pool[at, 1]


def attention_kernel(lay, js, first, last, ctl, *refs):
    refs = list(refs)
    take = lambda n: [refs.pop(0) for _ in range(n)]
    looped = len(js) > MAX_PERMUTES // 2
    qds = take(1 if looped else len(js))
    pool, slots, stats, mk, mv = take(5)
    if not first:
        prev = take(3)
    dqs = take(1 if looped else len(js))
    if last:
        local, own_mem = take(2)
        backs = take(lay.spans)
        acc, dmk, dmv, slot_pool, mkt = take(5)
    else:
        acc, dmk, dmv = take(3)
        slot_pool, mkt = take(2)
    heads = range(lay.heads)
    ways = lay.ways
    if first:
        for total in (acc, dmk, dmv):
            total[...] = jnp.zeros_like(total)
    else:
        for total, before in zip((acc, dmk, dmv), prev):
            total[...] = before[...]
    slot_pool[:ways] = pool[...]
    for s in range(lay.spans):
        slot_pool[ways + s, 0] = slots[s, 0]
        slot_pool[ways + s, 1] = slots[s, 1]
        slot_pool[ways + s, 2] = slots[s, 0].T
    for h in heads:
        mkt[h] = mk[:, col(h)].T

    def one_block(k, qd, dq):
        index, far = lay.pairs(ctl, k)
        stat = stats[partner(ctl[0], k, ways)]
        lse = jnp.concatenate([stat[h : h + 1] for h in heads], axis=1) * LOG2E
        delta = jnp.concatenate([stat[lay.heads + h : lay.heads + h + 1] for h in heads], axis=1)
        q_heads = [qd[0, :, col(h)] for h in heads]
        do_heads = [qd[1, :, col(h)] for h in heads]
        q_all = jnp.concatenate(q_heads, axis=0)
        do_all = jnp.concatenate(do_heads, axis=0)
        keys = jnp.concatenate([slot_pool[i, 0] for i in index], axis=0)
        values = jnp.concatenate([slot_pool[i, 1] for i in index], axis=0)
        keys_t = jnp.concatenate([slot_pool[i, 2] for i in index], axis=1)

        def weigh(scores, dweights, lse_row):
            weights = jnp.exp2(scores * (SCALE * LOG2E) - lse_row)
            dscores = weights * (dweights - delta)
            return weights.astype(jnp.bfloat16), dscores.astype(jnp.bfloat16)

        scores = dot(keys, q_all, NT)
        dweights = dot(values, do_all, NT)
        parts = []
        for j in range(SEQ_PAIRS):
            rows = slice(j * BLOCK, (j + 1) * BLOCK)
            parts.append(weigh(scores[rows], dweights[rows], lse + far[j]))
        weights = jnp.concatenate([w for w, _ in parts], axis=0)
        dscores = jnp.concatenate([d for _, d in parts], axis=0)
        dq_t = dot(keys_t, dscores)
        dk = dot(dscores, q_all)
        dv = dot(weights, do_all)
        for j, i in enumerate(index):
            rows = slice(j * BLOCK, (j + 1) * BLOCK)
            acc[i, 0] += dk[rows]
            acc[i, 1] += dv[rows]

        mem_scores = jnp.concatenate([dot(mk[:, col(h)], q_heads[h], NT) for h in heads], axis=1)
        mem_dweights = jnp.concatenate(
            [dot(mv[:, col(h)], do_heads[h], NT) for h in heads], axis=1
        )
        mem_w, mem_d = weigh(mem_scores, mem_dweights, lse)
        for h in heads:
            lanes = slice(h * HEAD_FEATURES, (h + 1) * HEAD_FEATURES)
            dmk[:, col(h)] += dot(mem_d[:, lanes], q_heads[h])
            dmv[:, col(h)] += dot(mem_w[:, lanes], do_heads[h])
            head_dq = dq_t[:, lanes] + dot(mkt[h], mem_d[:, lanes])
            dq[:, col(h)] = (head_dq * SCALE).T.astype(jnp.bfloat16)

    if looped:

        @pl.loop(0, len(js))
        def _(n):
            for i in range(2):
                one_block(2 * (js[0] + n) + i, qds[0].at[n, i], dqs[0].at[n, i])
    else:
        for j, qd, dq in zip(js, qds, dqs):
            for i in range(2):
                one_block(2 * j + i, qd.at[i], dq.at[i])

    if last:
        local[...] = acc[:ways]
        for k, back in enumerate(backs):
            span = partner(ctl[1], k, lay.spans)
            back[0] = (acc[ways + span, 0] * SCALE).astype(jnp.bfloat16)
            back[1] = acc[ways + span, 1].astype(jnp.bfloat16)
            for h in heads if lay.mem_rows else ():
                rows = pl.ds(pl.multiple_of(span * lay.mem_rows, lay.mem_rows), lay.mem_rows)
                at = pl.ds(h * lay.mem_rows, lay.mem_rows)
                back[2, at] = (dmk[rows, col(h)] * SCALE).astype(jnp.bfloat16)
                back[3, at] = dmv[rows, col(h)].astype(jnp.bfloat16)
        rows = slice(None)
        if lay.mem_rows:
            rows = pl.ds(pl.multiple_of(ctl[1] * lay.mem_rows, lay.mem_rows), lay.mem_rows)
        own_mem[0] = dmk[rows, :] * SCALE
        own_mem[1] = dmv[rows, :]


def attention(lay, js, ctl, qds, pool, slots, stats, mk, mv, before, last):
    blocks = lay.ways + lay.spans
    totals = [
        array((blocks, 2, BLOCK, HEAD_FEATURES), jnp.float32),
        array((BLOCK, lay.width), jnp.float32),
        array((BLOCK, lay.width), jnp.float32),
    ]
    scratch = [
        pltpu.VMEM((blocks, 3, BLOCK, HEAD_FEATURES), jnp.bfloat16),
        pltpu.VMEM((lay.heads, BLOCK, HEAD_FEATURES), jnp.bfloat16),
    ]
    pieces = [qds[j] for j in js]
    outs = [array((2, BLOCK, lay.width))] * len(js)
    looped = len(js) > MAX_PERMUTES // 2
    if looped:
        pieces = [jnp.stack(pieces)]
        outs = [array((len(js), 2, BLOCK, lay.width))]
    if last:
        outs += [
            array((lay.ways, 2, BLOCK, HEAD_FEATURES), jnp.float32),
            array((2, lay.mem_rows or BLOCK, lay.width), jnp.float32),
        ]
        outs += [array((4 if lay.mem_rows else 2, BLOCK, HEAD_FEATURES))] * lay.spans
        scratch = [pltpu.VMEM(t.shape, t.dtype) for t in totals] + scratch
    else:
        outs += totals
    done = call(
        functools.partial(attention_kernel, lay, js, before is None, last),
        outs,
        ctl,
        *pieces,
        pool,
        slots,
        stats,
        mk,
        mv,
        *(before or []),
        scratch=scratch,
    )
    dq = done[0] if looped else done[: len(js)]
    return dict(zip(js, dq)), done[1 if looped else len(js) :]


def merge_kernel(lay, ctl, local, own_mem, *refs):
    backs = refs[: lay.spans]
    *pieces, mem_sum, total = refs[lay.spans :]
    for k in range(lay.ways):
        total[k, 0] = local[k, 0] * SCALE
        total[k, 1] = local[k, 1]
    mem = [own_mem[0], own_mem[1]]
    for k, back in enumerate(backs):
        span = partner(ctl[1], k, lay.spans)

        @pl.when(span != ctl[1])
        def _():
            at = lay.send_index(ctl, span)
            for i in range(2):
                total[at, i] += back[i].astype(jnp.float32)

        if lay.mem_rows:
            for i in range(2):
                rows = [pl.ds(h * lay.mem_rows, lay.mem_rows) for h in range(lay.heads)]
                term = jnp.concatenate([back[2 + i, r] for r in rows], axis=1)
                mem[i] += jnp.where(span == ctl[1], 0.0, term.astype(jnp.float32))
    for s in range(mem_sum.shape[0]):
        for i in range(2):
            mem_sum[s, i] = mem[i]
    for j, piece in enumerate(pieces):
        for i in range(2):
            piece[i] = total[2 * j + i].astype(jnp.bfloat16)


def by_partner(refs):
    *pieces, others = refs
    for j, piece in enumerate(pieces):
        yield 2 * j, piece.at[0]
        yield 2 * j + 1, others.at[j]


def finish_kernel(lay, ctl, mem, *refs):
    *pieces, out_q, out_k, out_v, out_mk, out_mv = refs
    pieces, query_pieces = pieces[: len(pieces) // 2], pieces[len(pieces) // 2 :]
    for k, piece in by_partner(query_pieces):
        out_q[:, col(partner(ctl[0], k, lay.ways), lay.width)] = piece[...]
    shared = lay.heads < GROUP
    if shared:
        out_k[...] = jnp.zeros_like(out_k)
        out_v[...] = jnp.zeros_like(out_v)
    for k, piece in by_partner(pieces):
        at = col(lay.key_head(partner(ctl[0], k, lay.ways)))
        for i, out in enumerate((out_k, out_v)):
            term = piece[i].astype(jnp.float32)
            out[:, at] = out[:, at] + term if shared else term
    for s in range(mem.shape[0]):
        rows = pl.ds(s * mem.shape[2], mem.shape[2])
        out_mk[rows, :] = mem[s, 0]
        out_mv[rows, :] = mem[s, 1]


def whole_exchange(pieces):
    ways = 2 * len(pieces)
    order = partner(lax.axis_index("uly"), jnp.arange(ways, dtype=jnp.int32), ways)
    sent = jnp.concatenate(pieces)[order]
    got = lax.all_to_all(sent, "uly", 0, 0, tiled=True)[order]
    got = got.reshape(len(pieces), 2, *got.shape[1:])
    return [*got, got[:, 1]]


def shards(
    queries, keys, values, grad_out, row_lse, row_delta, pattern, memory_keys, memory_values
):
    lay = Layout(lax.axis_size("uly"), lax.axis_size("blk"))
    chips = lay.ways // 2
    in_stages = staged(lay.ways)
    place = jnp.stack([lax.axis_index("uly"), lax.axis_index("blk")]).astype(jnp.int32)
    ctl = jnp.concatenate([place, pattern.reshape(-1)])

    qd = by_chip(lambda device: device, place, queries, grad_out, lay.width)
    late = place
    kv = by_chip(lay.key_head, late, keys, values, HEAD_FEATURES)
    steps = [range(chips)]
    if in_stages:
        half = max(1, chips // 2)
        steps = [range(half), *([j] for j in range(half, chips))]
        for j in [*range(half, chips), *range(1, half)]:
            kv[j] = swap(kv[j], 2 * j)
        qd[half] = swap(qd[half], 2 * half)
        qd[1] = swap(qd[1], 2)
        kv[1:], qd[half + 1] = after(kv[1:], qd[half + 1])
        qd[half + 1] = swap(qd[half + 1], 2 * half + 2)
        first = (qd[1], qd[half])
        (qd[1], qd[half]), kv[0] = after(first, kv[0])
    pool, slots = call(
        functools.partial(pool_kernel, lay),
        [
            array((lay.ways, 3, BLOCK, HEAD_FEATURES)),
            array((lay.spans, 2, BLOCK, HEAD_FEATURES)),
        ],
        ctl,
        *kv,
    )
    slots = to_spans(slots)
    stats = jnp.concatenate([row_lse, row_delta], axis=1)
    stats = stats.reshape(lay.ways, BLOCK, 2 * lay.heads).transpose(0, 2, 1)

    totals, dq = None, {}
    for step in steps:
        last = step is steps[-1]
        step_dq, totals = attention(
            lay, step, ctl, qd, pool, slots, stats, memory_keys, memory_values, totals, last
        )
        dq |= step_dq
    local, own_mem, *backs = totals
    backs = across_spans(backs)
    if in_stages:
        for j in [*range(half, chips), *range(1, half)]:
            dq[j] = swap(dq[j], 2 * j)
        dq[half], backs = after(dq[half], backs)
    *dkv, mem = call(
        functools.partial(merge_kernel, lay),
        [array((2, 2, BLOCK, HEAD_FEATURES))] * chips
        + [array((lay.spans if lay.mem_rows else 1, *own_mem.shape), jnp.float32)],
        ctl,
        local,
        own_mem,
        *backs,
        scratch=[pltpu.VMEM((lay.ways, 2, BLOCK, HEAD_FEATURES), jnp.float32)],
    )
    mem = to_spans(mem) if lay.mem_rows else lax.psum(mem, "blk")
    dq = [dq[j] for j in range(chips)]
    if in_stages:
        (dq[1], dq[half + 1]), dkv = after((dq[1], dq[half + 1]), dkv)
        for j in [*range(half, chips), *range(1, half)]:
            dkv[j] = swap(dkv[j], 2 * j)
        (dkv[1:], mem), dq = after((dkv[1:], mem), dq)
        dq.append(to_blocks(dq))
        dkv.append(to_blocks(dkv))
    else:
        dq = whole_exchange(dq)
        dkv = whole_exchange(dkv)
    return tuple(call(
        functools.partial(finish_kernel, lay),
        [array(queries.shape)] + [array(keys.shape, jnp.float32)] * 2 + [array(memory_keys.shape, jnp.float32)] * 2,
        place,
        mem,
        *dkv,
        *dq,
    ))


def solution(mesh):
    in_specs = (
        P(("blk", "uly"), None),
        P(("blk", "uly"), None),
        P(("blk", "uly"), None),
        P(("blk", "uly"), None),
        P("blk", "uly"),
        P("blk", "uly"),
        P(),
        P(None, "uly"),
        P(None, "uly"),
    )
    out_specs = (
        P(("blk", "uly"), None),
        P(("blk", "uly"), None),
        P(("blk", "uly"), None),
        P(None, "uly"),
        P(None, "uly"),
    )
    return jax.shard_map(shards, mesh=mesh, in_specs=in_specs, out_specs=out_specs, check_vma=False)
```

```python
import functools
import math

import jax
import jax.numpy as jnp
from jax import lax
from jax.experimental import pallas as pl
from jax.experimental.pallas import tpu as pltpu
from jax.sharding import PartitionSpec as P

QUERY_HEADS = 32
KEY_HEADS = 8
HEAD_FEATURES = 128
BLOCK = 128
RANDOM = 2
SEQ_PAIRS = RANDOM + 3
GROUP = QUERY_HEADS // KEY_HEADS
SCALE = HEAD_FEATURES ** (-0.5)
LOG2E = math.log2(math.e)
FAR = 1e30
MAX_PERMUTES = 8
VMEM_LIMIT = 24 * 1024 * 1024
NN = (((1,), (0,)), ((), ()))
NT = (((1,), (1,)), ((), ()))
SMEM_SPEC = pl.BlockSpec(memory_space=pltpu.SMEM)


def dot(left, right, dims=NN):
    return lax.dot_general(left, right, dims, preferred_element_type=jnp.float32)


def col(at, width=HEAD_FEATURES):
    if isinstance(at, int):
        return pl.ds(at * width, width)
    return pl.ds(pl.multiple_of(at * width, width), width)


def even(n):
    return n & (n - 1) == 0


def partner(me, k, n):
    return me ^ k if even(n) else lax.rem(k - me + n, n)


def staged(n):
    return n == 8


def swap(piece, k):
    return lax.ppermute(piece, "uly", [(i, i ^ k) for i in range(lax.axis_size("uly"))])


def across_spans(pieces):
    spans = len(pieces)
    if even(spans) and spans <= MAX_PERMUTES:
        pairs = [[(i, i ^ k) for i in range(spans)] for k in range(spans)]
        return pieces[:1] + [lax.ppermute(pieces[k], "blk", pairs[k]) for k in range(1, spans)]
    order = partner(lax.axis_index("blk"), jnp.arange(spans, dtype=jnp.int32), spans)
    return list(to_spans(jnp.stack(pieces)[order])[order])


def to_spans(stacked):
    return lax.all_to_all(stacked, "blk", 0, 0, tiled=True)


def after(early, late):
    early, late = lax.optimization_barrier((early, late))
    return early, late


def call(kernel, outs, ctl, *operands, scratch=(), limit=VMEM_LIMIT):
    outputs = pl.pallas_call(
        kernel,
        in_specs=[SMEM_SPEC] + [pl.BlockSpec(memory_space=pltpu.VMEM)] * len(operands),
        out_specs=[pl.BlockSpec(memory_space=pltpu.VMEM)] * len(outs),
        out_shape=[jax.ShapeDtypeStruct(x.shape, x.dtype) for x in outs],
        scratch_shapes=list(scratch),
        compiler_params=pltpu.CompilerParams(vmem_limit_bytes=limit),
        cost_estimate=pl.CostEstimate(flops=0, bytes_accessed=0, transcendentals=0),
    )(ctl, *operands)
    return list(outputs)


def array(shape, dtype=jnp.bfloat16):
    return jax.ShapeDtypeStruct(shape, dtype)


class Layout:
    def __init__(self, ways, spans):
        self.ways = ways
        self.spans = spans
        self.heads = QUERY_HEADS // ways
        self.width = self.heads * HEAD_FEATURES
        self.mem_rows = BLOCK // spans if BLOCK % spans == 0 else 0

    def key_head(self, device):
        return lax.div(device * self.heads, GROUP)

    def pool_index(self, ctl, block):
        me, span = ctl[0], ctl[1]
        owner = lax.div(block, self.ways)
        local = lax.rem(block, self.ways)
        mine = partner(me, local, self.ways)
        return jnp.where(owner == span, mine, self.ways + owner)

    def pairs(self, ctl, k):
        me, span = ctl[0], ctl[1]
        block = span * self.ways + partner(me, k, self.ways)
        last = self.ways * self.spans - 1
        index = [
            self.pool_index(ctl, jnp.maximum(block - 1, 0)),
            self.pool_index(ctl, block),
            self.pool_index(ctl, jnp.minimum(block + 1, last)),
        ]
        index += [self.pool_index(ctl, ctl[2 + block * RANDOM + r]) for r in range(RANDOM)]
        far = [jnp.where(block == 0, FAR, 0.0), 0.0, jnp.where(block == last, FAR, 0.0)]
        return index, far + [0.0] * RANDOM

    def send_index(self, ctl, other):
        me, span = ctl[0], ctl[1]
        entries = self.ways * RANDOM

        def look(e, found):
            block = ctl[2 + other * entries + e]
            return jnp.where(lax.div(block, self.ways) == span, lax.rem(block, self.ways), found)

        named = lax.fori_loop(0, entries, look, jnp.int32(0))
        local = jnp.where(
            other == span + 1, self.ways - 1, jnp.where(other == span - 1, 0, named)
        )
        return partner(me, local, self.ways)


def cut_kernel(column, ks, ctl, first, second, out):
    for n, k in enumerate(ks):
        at = col(column(partner(ctl[0], k, lax.axis_size("uly"))), out.shape[3])
        out[n, 0] = first[:, at]
        out[n, 1] = second[:, at]


def cut(column, ks, ctl, first, second, width):
    out = array((len(ks), 2, BLOCK, width))
    return call(functools.partial(cut_kernel, column, ks), [out], ctl, first, second)[0]


def pack_kernel(column, ctl, first, second, got, *outs):
    for j, out in enumerate(outs):
        at = col(column(partner(ctl[0], 2 * j, lax.axis_size("uly"))), out.shape[3])
        out[0, 0] = first[:, at]
        out[0, 1] = second[:, at]
        out[1] = got[j]


def by_chip(column, ctl, first, second, width):
    ways = lax.axis_size("uly")
    chips = ways // 2
    if staged(ways):
        got = swap(cut(column, range(1, ways, 2), ctl, first, second, width), 1)
        return call(
            functools.partial(pack_kernel, column),
            [array((2, 2, BLOCK, width))] * chips,
            ctl,
            first,
            second,
            got,
        )
    order = partner(lax.axis_index("uly"), jnp.arange(ways, dtype=jnp.int32), ways)
    sent = cut(column, range(ways), ctl, first, second, width)[order]
    got = lax.all_to_all(sent, "uly", 0, 0, tiled=True)[order]
    return list(got.reshape(chips, 2, 2, BLOCK, width))


def pick_kernel(ctl, *refs):
    *pieces, out = refs
    for j, piece in enumerate(pieces):
        out[j] = piece[1]


def to_blocks(pieces):
    out = array((len(pieces), *pieces[0].shape[1:]), pieces[0].dtype)
    (other,) = call(pick_kernel, [out], jnp.zeros((1,), jnp.int32), *pieces)
    return swap(other, 1)


def pool_kernel(lay, ctl, *refs):
    *pieces, pool, slots = refs
    for j, piece in enumerate(pieces):
        for i in range(2):
            pool[2 * j + i, 0] = piece[i, 0]
            pool[2 * j + i, 1] = piece[i, 1]
            pool[2 * j + i, 2] = piece[i, 0].T
    for s in range(lay.spans):
        at = lay.send_index(ctl, s)
        slots[s, 0] = pool[at, 0]
        slots[s, 1] = pool[at, 1]


def attention_kernel(lay, js, first, last, ctl, *refs):
    refs = list(refs)
    take = lambda n: [refs.pop(0) for _ in range(n)]
    looped = len(js) > MAX_PERMUTES // 2
    qds = take(1 if looped else len(js))
    if first:
        pool, slots, stats, mk, mv = take(5)
    else:
        slot_pool, mkt, stats, mk, mv = take(5)
        prev = take(3)
    dqs = take(1 if looped else len(js))
    acc, dmk, dmv = take(3)
    if first:
        slot_pool, mkt = take(2)
    if last:
        (own_mem,) = take(1)
        backs = take(lay.spans)
    heads = range(lay.heads)
    ways = lay.ways
    if first:
        for total in (acc, dmk, dmv):
            total[...] = jnp.zeros_like(total)
        slot_pool[:ways] = pool[...]
        for s in range(lay.spans):
            slot_pool[ways + s, 0] = slots[s, 0]
            slot_pool[ways + s, 1] = slots[s, 1]
            slot_pool[ways + s, 2] = slots[s, 0].T
        for h in heads:
            mkt[h] = mk[:, col(h)].T
    else:
        for total, before in zip((acc, dmk, dmv), prev):
            total[...] = before[...]

    def one_block(k, qd, dq):
        index, far = lay.pairs(ctl, k)
        stat = stats[partner(ctl[0], k, ways)]
        lse = jnp.concatenate([stat[h : h + 1] for h in heads], axis=1) * LOG2E
        delta = jnp.concatenate([stat[lay.heads + h : lay.heads + h + 1] for h in heads], axis=1)
        q_heads = [qd[0, :, col(h)] for h in heads]
        do_heads = [qd[1, :, col(h)] for h in heads]
        q_all = jnp.concatenate(q_heads, axis=0)
        do_all = jnp.concatenate(do_heads, axis=0)
        keys = jnp.concatenate([slot_pool[i, 0] for i in index], axis=0)
        values = jnp.concatenate([slot_pool[i, 1] for i in index], axis=0)
        keys_t = jnp.concatenate([slot_pool[i, 2] for i in index], axis=1)

        def weigh(scores, dweights, lse_row):
            weights = jnp.exp2(scores * (SCALE * LOG2E) - lse_row)
            dscores = weights * (dweights - delta)
            return weights.astype(jnp.bfloat16), dscores.astype(jnp.bfloat16)

        scores = dot(keys, q_all, NT)
        dweights = dot(values, do_all, NT)
        parts = []
        for j in range(SEQ_PAIRS):
            rows = slice(j * BLOCK, (j + 1) * BLOCK)
            parts.append(weigh(scores[rows], dweights[rows], lse + far[j]))
        weights = jnp.concatenate([w for w, _ in parts], axis=0)
        dscores = jnp.concatenate([d for _, d in parts], axis=0)
        dq_t = dot(keys_t, dscores)
        dk = dot(dscores, q_all)
        dv = dot(weights, do_all)
        for j, i in enumerate(index):
            rows = slice(j * BLOCK, (j + 1) * BLOCK)
            acc[i, 0] += dk[rows]
            acc[i, 1] += dv[rows]

        mem_scores = jnp.concatenate([dot(mk[:, col(h)], q_heads[h], NT) for h in heads], axis=1)
        mem_dweights = jnp.concatenate(
            [dot(mv[:, col(h)], do_heads[h], NT) for h in heads], axis=1
        )
        mem_w, mem_d = weigh(mem_scores, mem_dweights, lse)
        for h in heads:
            lanes = slice(h * HEAD_FEATURES, (h + 1) * HEAD_FEATURES)
            dmk[:, col(h)] += dot(mem_d[:, lanes], q_heads[h])
            dmv[:, col(h)] += dot(mem_w[:, lanes], do_heads[h])
            head_dq = dq_t[:, lanes] + dot(mkt[h], mem_d[:, lanes])
            dq[:, col(h)] = (head_dq * SCALE).T.astype(jnp.bfloat16)

    if looped:

        @pl.loop(0, len(js))
        def _(n):
            for i in range(2):
                one_block(2 * (js[0] + n) + i, qds[0].at[n, i], dqs[0].at[n, i])
    else:
        for j, qd, dq in zip(js, qds, dqs):
            for i in range(2):
                one_block(2 * j + i, qd.at[i], dq.at[i])

    if last:
        for k, back in enumerate(backs):
            span = partner(ctl[1], k, lay.spans)
            back[0] = (acc[ways + span, 0] * SCALE).astype(jnp.bfloat16)
            back[1] = acc[ways + span, 1].astype(jnp.bfloat16)
            for h in heads if lay.mem_rows else ():
                rows = pl.ds(pl.multiple_of(span * lay.mem_rows, lay.mem_rows), lay.mem_rows)
                at = pl.ds(h * lay.mem_rows, lay.mem_rows)
                back[2, at] = (dmk[rows, col(h)] * SCALE).astype(jnp.bfloat16)
                back[3, at] = dmv[rows, col(h)].astype(jnp.bfloat16)
        rows = slice(None)
        if lay.mem_rows:
            rows = pl.ds(pl.multiple_of(ctl[1] * lay.mem_rows, lay.mem_rows), lay.mem_rows)
        own_mem[0] = dmk[rows, :] * SCALE
        own_mem[1] = dmv[rows, :]


def attention(lay, js, ctl, qds, pools, stats, mk, mv, before, last):
    blocks = lay.ways + lay.spans
    pieces = [qds[j] for j in js]
    dq = [array((2, BLOCK, lay.width))] * len(js)
    if len(js) > MAX_PERMUTES // 2:
        pieces = [jnp.stack(pieces)]
        dq = [array((len(js), 2, BLOCK, lay.width))]
    totals = [
        array((blocks, 2, BLOCK, HEAD_FEATURES), jnp.float32),
        array((BLOCK, lay.width), jnp.float32),
        array((BLOCK, lay.width), jnp.float32),
    ]
    whole = [
        array((blocks, 3, BLOCK, HEAD_FEATURES)),
        array((lay.heads, BLOCK, HEAD_FEATURES)),
    ]
    sent = [array((2, lay.mem_rows or BLOCK, lay.width), jnp.float32)]
    sent += [array((4 if lay.mem_rows else 2, BLOCK, HEAD_FEATURES))] * lay.spans
    first = before is None
    done = call(
        functools.partial(attention_kernel, lay, js, first, last),
        dq + totals + (whole if first else []) + (sent if last else []),
        ctl,
        *pieces,
        *pools,
        stats,
        mk,
        mv,
        *(before or []),
    )
    dq, done = done[: len(dq)], done[len(dq) :]
    totals, done = done[:3], done[3:]
    if first:
        pools, done = done[:2], done[2:]
    return dict(zip(js, dq if len(dq) == len(js) else dq[0])), totals, pools, done


def merge_kernel(lay, ctl, acc, own_mem, *refs):
    backs = refs[: lay.spans]
    *pieces, mem_sum, total = refs[lay.spans :]
    for k in range(lay.ways):
        total[k, 0] = acc[k, 0] * SCALE
        total[k, 1] = acc[k, 1]
    mem = [own_mem[0], own_mem[1]]
    for k, back in enumerate(backs):
        span = partner(ctl[1], k, lay.spans)

        @pl.when(span != ctl[1])
        def _():
            at = lay.send_index(ctl, span)
            for i in range(2):
                total[at, i] += back[i].astype(jnp.float32)

        if lay.mem_rows:
            for i in range(2):
                rows = [pl.ds(h * lay.mem_rows, lay.mem_rows) for h in range(lay.heads)]
                term = jnp.concatenate([back[2 + i, r] for r in rows], axis=1)
                mem[i] += jnp.where(span == ctl[1], 0.0, term.astype(jnp.float32))
    for s in range(mem_sum.shape[0]):
        for i in range(2):
            mem_sum[s, i] = mem[i]
    for j, piece in enumerate(pieces):
        for i in range(2):
            piece[i] = total[2 * j + i].astype(jnp.bfloat16)


def by_partner(refs):
    *pieces, others = refs
    for j, piece in enumerate(pieces):
        yield 2 * j, piece.at[0]
        yield 2 * j + 1, others.at[j]


def finish_kernel(lay, ctl, mem, *refs):
    *pieces, out_q, out_k, out_v, out_mk, out_mv = refs
    pieces, query_pieces = pieces[: len(pieces) // 2], pieces[len(pieces) // 2 :]
    for k, piece in by_partner(query_pieces):
        out_q[:, col(partner(ctl[0], k, lay.ways), lay.width)] = piece[...]
    shared = lay.heads < GROUP
    if shared:
        out_k[...] = jnp.zeros_like(out_k)
        out_v[...] = jnp.zeros_like(out_v)
    for k, piece in by_partner(pieces):
        at = col(lay.key_head(partner(ctl[0], k, lay.ways)))
        for i, out in enumerate((out_k, out_v)):
            term = piece[i].astype(jnp.float32)
            out[:, at] = out[:, at] + term if shared else term
    for s in range(mem.shape[0]):
        rows = pl.ds(s * mem.shape[2], mem.shape[2])
        out_mk[rows, :] = mem[s, 0]
        out_mv[rows, :] = mem[s, 1]


def whole_exchange(pieces):
    ways = 2 * len(pieces)
    order = partner(lax.axis_index("uly"), jnp.arange(ways, dtype=jnp.int32), ways)
    sent = jnp.concatenate(pieces)[order]
    got = lax.all_to_all(sent, "uly", 0, 0, tiled=True)[order]
    got = got.reshape(len(pieces), 2, *got.shape[1:])
    return [*got, got[:, 1]]


def shards(
    queries, keys, values, grad_out, row_lse, row_delta, pattern, memory_keys, memory_values
):
    lay = Layout(lax.axis_size("uly"), lax.axis_size("blk"))
    chips = lay.ways // 2
    in_stages = staged(lay.ways)
    place = jnp.stack([lax.axis_index("uly"), lax.axis_index("blk")]).astype(jnp.int32)
    ctl = jnp.concatenate([place, pattern.reshape(-1)])

    qd = by_chip(lambda device: device, place, queries, grad_out, lay.width)
    kv = by_chip(lay.key_head, place, keys, values, HEAD_FEATURES)
    steps = [range(chips)]
    if in_stages:
        half = max(1, chips // 2)
        far, last_far = 3, 2
        steps = [range(half), [far], [last_far]]
        for j in [far, last_far, 1]:
            kv[j] = swap(kv[j], 2 * j)
        qd[far] = swap(qd[far], 2 * far)
        qd[1] = swap(qd[1], 2)
        kv[1:], qd[last_far] = after(kv[1:], qd[last_far])
        qd[last_far] = swap(qd[last_far], 2 * last_far)
        (qd[1], qd[far]), kv[0] = after((qd[1], qd[far]), kv[0])
    pool, slots = call(
        functools.partial(pool_kernel, lay),
        [
            array((lay.ways, 3, BLOCK, HEAD_FEATURES)),
            array((lay.spans, 2, BLOCK, HEAD_FEATURES)),
        ],
        ctl,
        *kv,
    )
    slots = to_spans(slots)
    stats = jnp.concatenate([row_lse, row_delta], axis=1)
    stats = stats.reshape(lay.ways, BLOCK, 2 * lay.heads).transpose(0, 2, 1)

    totals, pools, dq = None, (pool, slots), {}
    for step in steps:
        last = step is steps[-1]
        step_dq, totals, pools, sent = attention(
            lay, step, ctl, qd, pools, stats, memory_keys, memory_values, totals, last
        )
        dq |= step_dq
    own_mem, *backs = sent
    backs = across_spans(backs)
    if in_stages:
        for j in [far, last_far, 1]:
            dq[j] = swap(dq[j], 2 * j)
        dq[far], backs = after(dq[far], backs)
    *dkv, mem = call(
        functools.partial(merge_kernel, lay),
        [array((2, 2, BLOCK, HEAD_FEATURES))] * chips
        + [array((lay.spans if lay.mem_rows else 1, *own_mem.shape), jnp.float32)],
        ctl,
        totals[0],
        own_mem,
        *backs,
        scratch=[pltpu.VMEM((lay.ways, 2, BLOCK, HEAD_FEATURES), jnp.float32)],
    )
    mem = to_spans(mem) if lay.mem_rows else lax.psum(mem, "blk")
    dq = [dq[j] for j in range(chips)]
    if in_stages:
        (dq[1], dq[last_far]), dkv = after((dq[1], dq[last_far]), dkv)
        for j in [far, last_far, 1]:
            dkv[j] = swap(dkv[j], 2 * j)
        (dkv[1:], mem), dq = after((dkv[1:], mem), dq)
        dq.append(to_blocks(dq))
        dkv.append(to_blocks(dkv))
    else:
        dq = whole_exchange(dq)
        dkv = whole_exchange(dkv)
    outs = [queries.shape, keys.shape, keys.shape, memory_keys.shape, memory_keys.shape]
    kinds = [jnp.bfloat16] + [jnp.float32] * 4
    outs = [array(shape, kind) for shape, kind in zip(outs, kinds)]
    return tuple(call(functools.partial(finish_kernel, lay), outs, place, mem, *dkv, *dq))


def solution(mesh):
    in_specs = (
        P(("blk", "uly"), None),
        P(("blk", "uly"), None),
        P(("blk", "uly"), None),
        P(("blk", "uly"), None),
        P("blk", "uly"),
        P("blk", "uly"),
        P(),
        P(None, "uly"),
        P(None, "uly"),
    )
    out_specs = (
        P(("blk", "uly"), None),
        P(("blk", "uly"), None),
        P(("blk", "uly"), None),
        P(None, "uly"),
        P(None, "uly"),
    )
    return jax.shard_map(shards, mesh=mesh, in_specs=in_specs, out_specs=out_specs, check_vma=False)
```

```python
import functools
import math

import jax
import jax.numpy as jnp
from jax import lax
from jax.experimental import pallas as pl
from jax.experimental.pallas import tpu as pltpu
from jax.sharding import PartitionSpec as P

QUERY_HEADS = 32
KEY_HEADS = 8
HEAD_FEATURES = 128
BLOCK = 128
RANDOM = 2
SEQ_PAIRS = RANDOM + 3
GROUP = QUERY_HEADS // KEY_HEADS
SCALE = HEAD_FEATURES ** (-0.5)
LOG2E = math.log2(math.e)
FAR = 1e30
MAX_PERMUTES = 8
VMEM_LIMIT = 24 * 1024 * 1024
NN = (((1,), (0,)), ((), ()))
NT = (((1,), (1,)), ((), ()))
SMEM_SPEC = pl.BlockSpec(memory_space=pltpu.SMEM)


def dot(left, right, dims=NN):
    return lax.dot_general(left, right, dims, preferred_element_type=jnp.float32)


def col(at, width=HEAD_FEATURES):
    if isinstance(at, int):
        return pl.ds(at * width, width)
    return pl.ds(pl.multiple_of(at * width, width), width)


def even(n):
    return n & (n - 1) == 0


def partner(me, k, n):
    return me ^ k if even(n) else lax.rem(k - me + n, n)


def staged(n):
    return n == 8


def swap(piece, k):
    return lax.ppermute(piece, "uly", [(i, i ^ k) for i in range(lax.axis_size("uly"))])


def across_spans(pieces):
    spans = len(pieces)
    if even(spans) and spans <= MAX_PERMUTES:
        pairs = [[(i, i ^ k) for i in range(spans)] for k in range(spans)]
        return pieces[:1] + [lax.ppermute(pieces[k], "blk", pairs[k]) for k in range(1, spans)]
    order = partner(lax.axis_index("blk"), jnp.arange(spans, dtype=jnp.int32), spans)
    return list(to_spans(jnp.stack(pieces)[order])[order])


def to_spans(stacked):
    return lax.all_to_all(stacked, "blk", 0, 0, tiled=True)


def after(early, late):
    early, late = lax.optimization_barrier((early, late))
    return early, late


def call(kernel, outs, ctl, *operands, scratch=(), limit=VMEM_LIMIT):
    outputs = pl.pallas_call(
        kernel,
        in_specs=[SMEM_SPEC] + [pl.BlockSpec(memory_space=pltpu.VMEM)] * len(operands),
        out_specs=[pl.BlockSpec(memory_space=pltpu.VMEM)] * len(outs),
        out_shape=[jax.ShapeDtypeStruct(x.shape, x.dtype) for x in outs],
        scratch_shapes=list(scratch),
        compiler_params=pltpu.CompilerParams(vmem_limit_bytes=limit),
        cost_estimate=pl.CostEstimate(flops=0, bytes_accessed=0, transcendentals=0),
    )(ctl, *operands)
    return list(outputs)


def array(shape, dtype=jnp.bfloat16):
    return jax.ShapeDtypeStruct(shape, dtype)


class Layout:
    def __init__(self, ways, spans):
        self.ways = ways
        self.spans = spans
        self.heads = QUERY_HEADS // ways
        self.width = self.heads * HEAD_FEATURES
        self.mem_rows = BLOCK // spans if BLOCK % spans == 0 else 0

    def key_head(self, device):
        return lax.div(device * self.heads, GROUP)

    def pool_index(self, ctl, block):
        me, span = ctl[0], ctl[1]
        owner = lax.div(block, self.ways)
        local = lax.rem(block, self.ways)
        mine = partner(me, local, self.ways)
        return jnp.where(owner == span, mine, self.ways + owner)

    def pairs(self, ctl, k):
        me, span = ctl[0], ctl[1]
        block = span * self.ways + partner(me, k, self.ways)
        last = self.ways * self.spans - 1
        index = [
            self.pool_index(ctl, jnp.maximum(block - 1, 0)),
            self.pool_index(ctl, block),
            self.pool_index(ctl, jnp.minimum(block + 1, last)),
        ]
        index += [self.pool_index(ctl, ctl[2 + block * RANDOM + r]) for r in range(RANDOM)]
        far = [jnp.where(block == 0, FAR, 0.0), 0.0, jnp.where(block == last, FAR, 0.0)]
        return index, far + [0.0] * RANDOM

    def send_index(self, ctl, other):
        me, span = ctl[0], ctl[1]
        entries = self.ways * RANDOM

        def look(e, found):
            block = ctl[2 + other * entries + e]
            return jnp.where(lax.div(block, self.ways) == span, lax.rem(block, self.ways), found)

        named = lax.fori_loop(0, entries, look, jnp.int32(0))
        local = jnp.where(
            other == span + 1, self.ways - 1, jnp.where(other == span - 1, 0, named)
        )
        return partner(me, local, self.ways)


def cut_kernel(column, ks, ctl, first, second, out):
    for n, k in enumerate(ks):
        at = col(column(partner(ctl[0], k, lax.axis_size("uly"))), out.shape[3])
        out[n, 0] = first[:, at]
        out[n, 1] = second[:, at]


def cut(column, ks, ctl, first, second, width):
    out = array((len(ks), 2, BLOCK, width))
    return call(functools.partial(cut_kernel, column, ks), [out], ctl, first, second)[0]


def pack_kernel(column, ctl, first, second, got, *outs):
    for j, out in enumerate(outs):
        at = col(column(partner(ctl[0], 2 * j, lax.axis_size("uly"))), out.shape[3])
        out[0, 0] = first[:, at]
        out[0, 1] = second[:, at]
        out[1] = got[j]


def by_chip(column, ctl, first, second, width):
    ways = lax.axis_size("uly")
    chips = ways // 2
    if staged(ways):
        got = swap(cut(column, range(1, ways, 2), ctl, first, second, width), 1)
        return call(
            functools.partial(pack_kernel, column),
            [array((2, 2, BLOCK, width))] * chips,
            ctl,
            first,
            second,
            got,
        )
    order = partner(lax.axis_index("uly"), jnp.arange(ways, dtype=jnp.int32), ways)
    sent = cut(column, range(ways), ctl, first, second, width)[order]
    got = lax.all_to_all(sent, "uly", 0, 0, tiled=True)[order]
    return list(got.reshape(chips, 2, 2, BLOCK, width))


def pick_kernel(ctl, *refs):
    *pieces, out = refs
    for j, piece in enumerate(pieces):
        out[j] = piece[1]


def to_blocks(pieces):
    out = array((len(pieces), *pieces[0].shape[1:]), pieces[0].dtype)
    (other,) = call(pick_kernel, [out], jnp.zeros((1,), jnp.int32), *pieces)
    return swap(other, 1)


def pool_kernel(lay, ctl, *refs):
    pieces, pool, slots = refs[: lay.ways // 2], refs[lay.ways // 2], refs[lay.ways // 2 + 1 :]
    for j, piece in enumerate(pieces):
        for i in range(2):
            pool[2 * j + i, 0] = piece[i, 0]
            pool[2 * j + i, 1] = piece[i, 1]
            pool[2 * j + i, 2] = piece[i, 0].T
    for k, slot in enumerate(slots):
        at = lay.send_index(ctl, partner(ctl[1], k, lay.spans))
        slot[0] = pool[at, 0]
        slot[1] = pool[at, 1]


def attention_kernel(lay, js, first, last, ctl, *refs):
    refs = list(refs)
    take = lambda n: [refs.pop(0) for _ in range(n)]
    looped = len(js) > MAX_PERMUTES // 2
    qds = take(1 if looped else len(js))
    if first:
        (pool,) = take(1)
        slots = take(lay.spans)
        stats, mk, mv = take(3)
    else:
        slot_pool, mkt, stats, mk, mv = take(5)
        prev = take(3)
    dqs = take(1 if looped else len(js))
    acc, dmk, dmv = take(3)
    if first:
        slot_pool, mkt = take(2)
    if last:
        (own_mem,) = take(1)
        backs = take(lay.spans)
    heads = range(lay.heads)
    ways = lay.ways
    if first:
        for total in (acc, dmk, dmv):
            total[...] = jnp.zeros_like(total)
        slot_pool[:ways] = pool[...]
        for k, slot in enumerate(slots):
            at = ways + partner(ctl[1], k, lay.spans)
            slot_pool[at, 0] = slot[0]
            slot_pool[at, 1] = slot[1]
            slot_pool[at, 2] = slot[0].T
        for h in heads:
            mkt[h] = mk[:, col(h)].T
    else:
        for total, before in zip((acc, dmk, dmv), prev):
            total[...] = before[...]

    def one_block(k, qd, dq):
        index, far = lay.pairs(ctl, k)
        stat = stats[partner(ctl[0], k, ways)]
        lse = jnp.concatenate([stat[h : h + 1] for h in heads], axis=1) * LOG2E
        delta = jnp.concatenate([stat[lay.heads + h : lay.heads + h + 1] for h in heads], axis=1)
        q_heads = [qd[0, :, col(h)] for h in heads]
        do_heads = [qd[1, :, col(h)] for h in heads]
        q_all = jnp.concatenate(q_heads, axis=0)
        do_all = jnp.concatenate(do_heads, axis=0)
        keys = jnp.concatenate([slot_pool[i, 0] for i in index], axis=0)
        values = jnp.concatenate([slot_pool[i, 1] for i in index], axis=0)
        keys_t = jnp.concatenate([slot_pool[i, 2] for i in index], axis=1)

        def weigh(scores, dweights, lse_row):
            weights = jnp.exp2(scores * (SCALE * LOG2E) - lse_row)
            dscores = weights * (dweights - delta)
            return weights.astype(jnp.bfloat16), dscores.astype(jnp.bfloat16)

        scores = dot(keys, q_all, NT)
        dweights = dot(values, do_all, NT)
        parts = []
        for j in range(SEQ_PAIRS):
            rows = slice(j * BLOCK, (j + 1) * BLOCK)
            parts.append(weigh(scores[rows], dweights[rows], lse + far[j]))
        weights = jnp.concatenate([w for w, _ in parts], axis=0)
        dscores = jnp.concatenate([d for _, d in parts], axis=0)
        dq_t = dot(keys_t, dscores)
        dk = dot(dscores, q_all)
        dv = dot(weights, do_all)
        for j, i in enumerate(index):
            rows = slice(j * BLOCK, (j + 1) * BLOCK)
            acc[i, 0] += dk[rows]
            acc[i, 1] += dv[rows]

        mem_scores = jnp.concatenate([dot(mk[:, col(h)], q_heads[h], NT) for h in heads], axis=1)
        mem_dweights = jnp.concatenate(
            [dot(mv[:, col(h)], do_heads[h], NT) for h in heads], axis=1
        )
        mem_w, mem_d = weigh(mem_scores, mem_dweights, lse)
        for h in heads:
            lanes = slice(h * HEAD_FEATURES, (h + 1) * HEAD_FEATURES)
            dmk[:, col(h)] += dot(mem_d[:, lanes], q_heads[h])
            dmv[:, col(h)] += dot(mem_w[:, lanes], do_heads[h])
            head_dq = dq_t[:, lanes] + dot(mkt[h], mem_d[:, lanes])
            dq[:, col(h)] = (head_dq * SCALE).T.astype(jnp.bfloat16)

    if looped:

        @pl.loop(0, len(js))
        def _(n):
            for i in range(2):
                one_block(2 * (js[0] + n) + i, qds[0].at[n, i], dqs[0].at[n, i])
    else:
        for j, qd, dq in zip(js, qds, dqs):
            for i in range(2):
                one_block(2 * j + i, qd.at[i], dq.at[i])

    if last:
        for k, back in enumerate(backs):
            span = partner(ctl[1], k, lay.spans)
            back[0] = (acc[ways + span, 0] * SCALE).astype(jnp.bfloat16)
            back[1] = acc[ways + span, 1].astype(jnp.bfloat16)
            for h in heads if lay.mem_rows else ():
                rows = pl.ds(pl.multiple_of(span * lay.mem_rows, lay.mem_rows), lay.mem_rows)
                at = pl.ds(h * lay.mem_rows, lay.mem_rows)
                back[2, at] = (dmk[rows, col(h)] * SCALE).astype(jnp.bfloat16)
                back[3, at] = dmv[rows, col(h)].astype(jnp.bfloat16)
        rows = slice(None)
        if lay.mem_rows:
            rows = pl.ds(pl.multiple_of(ctl[1] * lay.mem_rows, lay.mem_rows), lay.mem_rows)
        own_mem[0] = dmk[rows, :] * SCALE
        own_mem[1] = dmv[rows, :]


def attention(lay, js, ctl, qds, pools, stats, mk, mv, before, last):
    blocks = lay.ways + lay.spans
    pieces = [qds[j] for j in js]
    dq = [array((2, BLOCK, lay.width))] * len(js)
    if len(js) > MAX_PERMUTES // 2:
        pieces = [jnp.stack(pieces)]
        dq = [array((len(js), 2, BLOCK, lay.width))]
    totals = [
        array((blocks, 2, BLOCK, HEAD_FEATURES), jnp.float32),
        array((BLOCK, lay.width), jnp.float32),
        array((BLOCK, lay.width), jnp.float32),
    ]
    whole = [
        array((blocks, 3, BLOCK, HEAD_FEATURES)),
        array((lay.heads, BLOCK, HEAD_FEATURES)),
    ]
    sent = [array((2, lay.mem_rows or BLOCK, lay.width), jnp.float32)]
    sent += [array((4 if lay.mem_rows else 2, BLOCK, HEAD_FEATURES))] * lay.spans
    first = before is None
    done = call(
        functools.partial(attention_kernel, lay, js, first, last),
        dq + totals + (whole if first else []) + (sent if last else []),
        ctl,
        *pieces,
        *pools,
        stats,
        mk,
        mv,
        *(before or []),
    )
    dq, done = done[: len(dq)], done[len(dq) :]
    totals, done = done[:3], done[3:]
    if first:
        pools, done = done[:2], done[2:]
    return dict(zip(js, dq if len(dq) == len(js) else dq[0])), totals, pools, done


def merge_kernel(lay, ctl, acc, own_mem, *refs):
    backs = refs[: lay.spans]
    *pieces, mem_sum, total = refs[lay.spans :]
    for k in range(lay.ways):
        total[k, 0] = acc[k, 0] * SCALE
        total[k, 1] = acc[k, 1]
    mem = [own_mem[0], own_mem[1]]
    for k, back in enumerate(backs):
        span = partner(ctl[1], k, lay.spans)

        @pl.when(span != ctl[1])
        def _():
            at = lay.send_index(ctl, span)
            for i in range(2):
                total[at, i] += back[i].astype(jnp.float32)

        if lay.mem_rows:
            for i in range(2):
                rows = [pl.ds(h * lay.mem_rows, lay.mem_rows) for h in range(lay.heads)]
                term = jnp.concatenate([back[2 + i, r] for r in rows], axis=1)
                mem[i] += jnp.where(span == ctl[1], 0.0, term.astype(jnp.float32))
    for s in range(mem_sum.shape[0]):
        for i in range(2):
            mem_sum[s, i] = mem[i]
    for j, piece in enumerate(pieces):
        for i in range(2):
            piece[i] = total[2 * j + i].astype(jnp.bfloat16)


def by_partner(refs):
    *pieces, others = refs
    for j, piece in enumerate(pieces):
        yield 2 * j, piece.at[0]
        yield 2 * j + 1, others.at[j]


def finish_kernel(lay, ctl, mem, *refs):
    *pieces, out_q, out_k, out_v, out_mk, out_mv = refs
    pieces, query_pieces = pieces[: len(pieces) // 2], pieces[len(pieces) // 2 :]
    for k, piece in by_partner(query_pieces):
        out_q[:, col(partner(ctl[0], k, lay.ways), lay.width)] = piece[...]
    shared = lay.heads < GROUP
    if shared:
        out_k[...] = jnp.zeros_like(out_k)
        out_v[...] = jnp.zeros_like(out_v)
    for k, piece in by_partner(pieces):
        at = col(lay.key_head(partner(ctl[0], k, lay.ways)))
        for i, out in enumerate((out_k, out_v)):
            term = piece[i].astype(jnp.float32)
            out[:, at] = out[:, at] + term if shared else term
    for s in range(mem.shape[0]):
        rows = pl.ds(s * mem.shape[2], mem.shape[2])
        out_mk[rows, :] = mem[s, 0]
        out_mv[rows, :] = mem[s, 1]


def whole_exchange(pieces):
    ways = 2 * len(pieces)
    order = partner(lax.axis_index("uly"), jnp.arange(ways, dtype=jnp.int32), ways)
    sent = jnp.concatenate(pieces)[order]
    got = lax.all_to_all(sent, "uly", 0, 0, tiled=True)[order]
    got = got.reshape(len(pieces), 2, *got.shape[1:])
    return [*got, got[:, 1]]


def shards(
    queries, keys, values, grad_out, row_lse, row_delta, pattern, memory_keys, memory_values
):
    lay = Layout(lax.axis_size("uly"), lax.axis_size("blk"))
    chips = lay.ways // 2
    in_stages = staged(lay.ways)
    place = jnp.stack([lax.axis_index("uly"), lax.axis_index("blk")]).astype(jnp.int32)
    ctl = jnp.concatenate([place, pattern.reshape(-1)])

    qd = by_chip(lambda device: device, place, queries, grad_out, lay.width)
    kv = by_chip(lay.key_head, place, keys, values, HEAD_FEATURES)
    steps = [range(chips)]
    if in_stages:
        half = max(1, chips // 2)
        far, last_far = 3, 2
        steps = [range(half), [far], [last_far]]
        for j in [far, last_far, 1]:
            kv[j] = swap(kv[j], 2 * j)
        qd[far] = swap(qd[far], 2 * far)
        qd[1] = swap(qd[1], 2)
        kv[1:], qd[last_far] = after(kv[1:], qd[last_far])
        qd[last_far] = swap(qd[last_far], 2 * last_far)
        (qd[1], qd[far]), kv[0] = after((qd[1], qd[far]), kv[0])
    pool, *slots = call(
        functools.partial(pool_kernel, lay),
        [
            array((lay.ways, 3, BLOCK, HEAD_FEATURES)),
            *[array((2, BLOCK, HEAD_FEATURES))] * lay.spans,
        ],
        ctl,
        *kv,
    )
    slots = across_spans(slots)
    stats = jnp.concatenate([row_lse, row_delta], axis=1)
    stats = stats.reshape(lay.ways, BLOCK, 2 * lay.heads).transpose(0, 2, 1)

    totals, pools, dq = None, (pool, *slots), {}
    for step in steps:
        last = step is steps[-1]
        step_dq, totals, pools, sent = attention(
            lay, step, ctl, qd, pools, stats, memory_keys, memory_values, totals, last
        )
        dq |= step_dq
    own_mem, *backs = sent
    backs = across_spans(backs)
    if in_stages:
        for j in [far, last_far, 1]:
            dq[j] = swap(dq[j], 2 * j)
        dq[far], backs = after(dq[far], backs)
    *dkv, mem = call(
        functools.partial(merge_kernel, lay),
        [array((2, 2, BLOCK, HEAD_FEATURES))] * chips
        + [array((lay.spans if lay.mem_rows else 1, *own_mem.shape), jnp.float32)],
        ctl,
        totals[0],
        own_mem,
        *backs,
        scratch=[pltpu.VMEM((lay.ways, 2, BLOCK, HEAD_FEATURES), jnp.float32)],
    )
    mem = to_spans(mem) if lay.mem_rows else lax.psum(mem, "blk")
    dq = [dq[j] for j in range(chips)]
    if in_stages:
        (dq[1], dq[last_far]), dkv = after((dq[1], dq[last_far]), dkv)
        for j in [far, last_far, 1]:
            dkv[j] = swap(dkv[j], 2 * j)
        (dkv[1:], mem), dq = after((dkv[1:], mem), dq)
        dq.append(to_blocks(dq))
        dkv.append(to_blocks(dkv))
    else:
        dq = whole_exchange(dq)
        dkv = whole_exchange(dkv)
    outs = [queries.shape, keys.shape, keys.shape, memory_keys.shape, memory_keys.shape]
    kinds = [jnp.bfloat16] + [jnp.float32] * 4
    outs = [array(shape, kind) for shape, kind in zip(outs, kinds)]
    return tuple(call(functools.partial(finish_kernel, lay), outs, place, mem, *dkv, *dq))


def solution(mesh):
    in_specs = (
        P(("blk", "uly"), None),
        P(("blk", "uly"), None),
        P(("blk", "uly"), None),
        P(("blk", "uly"), None),
        P("blk", "uly"),
        P("blk", "uly"),
        P(),
        P(None, "uly"),
        P(None, "uly"),
    )
    out_specs = (
        P(("blk", "uly"), None),
        P(("blk", "uly"), None),
        P(("blk", "uly"), None),
        P(None, "uly"),
        P(None, "uly"),
    )
    return jax.shard_map(shards, mesh=mesh, in_specs=in_specs, out_specs=out_specs, check_vma=False)
```
